32 devices in a mesh: dp: 4 (over z), heads: 4 (over x, core), ctx: 2 (over y).
Axes of the slice: x: 2, y: 2, z: 4, core: 2. Of those that a mesh axis runs over, the one named last changes fastest.
Arguments:
- inputs: bfloat16 [4, 512, 5120], P('dp', 'ctx'), may hold values from -6 to 6
- queries: bfloat16 [4, 512, 4096], P('dp', 'ctx', 'heads'), may hold values from -6 to 6
- keys: bfloat16 [4, 512, 512], P('dp', 'ctx', 'heads'), may hold values from -6 to 6
- values: bfloat16 [4, 512, 512], P('dp', 'ctx', 'heads'), may hold values from -6 to 6
- outputs: bfloat16 [4, 512, 4096], P('dp', 'ctx', 'heads'), may hold values from -6 to 6
- out_grad: bfloat16 [4, 512, 4096], P('dp', 'ctx', 'heads'), may hold values from -6 to 6
- lse: float32 [4, 512, 32], P('dp', 'ctx', 'heads'), may hold values from 6 to 9
- positions: int32 [4, 512], P('dp', 'ctx'), may hold values from 0 to 511, as said below
Outputs:
- query_grad: float32 [4, 512, 4096], P('dp', 'ctx', 'heads')
- key_grad: float32 [4, 512, 512], P('dp', 'ctx', 'heads')
- value_grad: float32 [4, 512, 512], P('dp', 'ctx', 'heads')
- weight_grad: float32 [5120, 1024], P(('dp', 'ctx'), 'heads')
The draws below stay inside these ranges and needn't reach their ends.
Inputs may be any that keep to these rules, and one draw needn't show every extreme that they name: Each sequence's positions are a permutation of 0 to 511 made of 4 runs of 128 rising consecutive positions; each run fills an aligned block of 128 slots and starts at a multiple of 128.
All inputs are finite; a program needn't handle non-finite values.
Results may differ from the reference program's by a relative error of at most 0.0045.
Values may be sent and summed in bfloat16 or wider, within the bound.
A program may use at most 64 MiB of HBM per device.

```python
import jax
import jax.numpy as jnp
from jax import lax

D = 5120
HD = 128
GROUP = 8
KV_HEADS = 4
TOK_DEV = 256
L = 512
SEQS = 4
Q_HEADS = 32


def draw_positions(key, part):
    key = jax.random.fold_in(key, 5)
    half = TOK_DEV // 2
    count = L // half
    seq_keys = jax.random.split(key, SEQS)
    order = jax.vmap(lambda one_key: jax.random.permutation(one_key, count))(seq_keys)
    places = order[:, :, None] * half + jnp.arange(half, dtype=jnp.int32)[None, None, :]
    return places.reshape(SEQS, L).astype(jnp.int32)


def spiked(entries, stream_key, source, target, blocks, factor):
    def block_of(dim):
        return (jnp.arange(entries.shape[dim]) // (entries.shape[dim] // blocks)).reshape((-1,) + (1,) * (entries.ndim - 1 - dim))

    first = jax.random.permutation(stream_key, blocks)[block_of(target)]
    far = (block_of(target) + blocks // 2) % blocks
    return jnp.where((block_of(source) == first) | (block_of(source) == far), factor * entries, entries)


def steps_of(rng, shape, shards, low, largest):
    gain = 1.0
    for dim, blocks in shards:
        draws = jax.random.uniform(jax.random.fold_in(jax.random.fold_in(rng, 6), dim), (blocks,), jnp.float32, low / len(shards), largest / len(shards))
        gain = gain * jnp.repeat(jnp.exp(draws), shape[dim] // blocks).reshape((-1,) + (1,) * (len(shape) - 1 - dim))
    return gain


def centred(key, extent, scale, reach, cuts=(), kind=jnp.bfloat16):
    entries = scale * jax.random.normal(key, extent, jnp.float32)
    if cuts:
        entries = entries * steps_of(key, extent, cuts, -0.22, 0.18)
    return jnp.clip(entries, -reach, reach).astype(kind)


def bell_draw_with(key, shape, deviation, limit, cuts, heavy, kind=jnp.bfloat16):
    drawn = deviation * jax.random.normal(key, shape, jnp.float32)
    if cuts:
        drawn = drawn * steps_of(key, shape, cuts, -0.22, 0.18)
    return jnp.clip(spiked(drawn, jax.random.fold_in(key, 3), *heavy), -limit, limit).astype(kind)


def setup_inputs(seed: int = 0) -> dict:
    splits = jax.random.split(jax.random.key(seed), 9)
    return {
        "inputs": bell_draw_with(splits[0], (SEQS, L, D), 1.0, 6.0, ((0, 4), (1, 2)), (1, 2, 2, 2.0)),
        "queries": centred(splits[1], (SEQS, L, Q_HEADS * HD), 1.0, 6.0, ((0, 4), (1, 2), (2, 4))),
        "keys": centred(splits[2], (SEQS, L, KV_HEADS * HD), 1.0, 6.0, ((0, 4), (1, 2), (2, 4))),
        "values": centred(splits[3], (SEQS, L, KV_HEADS * HD), 1.0, 6.0, ((0, 4), (1, 2), (2, 4))),
        "outputs": centred(splits[4], (SEQS, L, Q_HEADS * HD), 1.0, 6.0, ((0, 4), (1, 2), (2, 4))),
        "out_grad": centred(splits[5], (SEQS, L, Q_HEADS * HD), 1.0, 6.0, ((0, 4), (1, 2), (2, 4))),
        "lse": jnp.clip(6.0 + 3.0 * jax.random.uniform(splits[6], (SEQS, L, Q_HEADS), jnp.float32) ** steps_of(splits[6], (SEQS, L, Q_HEADS), ((0, 4), (1, 2), (2, 4)), -0.2, 0.2), 6.0, 9.0),
        "positions": draw_positions(jax.random.fold_in(splits[8], 71), 0),
    }


def group_grads(query_g, key_g, value_g, grad_g, out_g, lse_g, visible):
    factor = HD ** -0.5
    query_f = query_g.reshape(L, GROUP, HD).astype(jnp.float32)
    grad_f = grad_g.reshape(L, GROUP, HD).astype(jnp.float32)
    out_f = out_g.reshape(L, GROUP, HD).astype(jnp.float32)
    key_f = key_g.astype(jnp.float32)
    value_f = value_g.astype(jnp.float32)
    delta = jnp.sum(grad_f * out_f, axis=2)
    scores = jnp.einsum("qgd,kd->gqk", query_f, key_f) * factor
    probs = jnp.where(visible[None], jnp.exp(scores - jnp.transpose(lse_g)[:, :, None]), jnp.float32(0.0))
    dprobs = jnp.einsum("qgd,kd->gqk", grad_f, value_f)
    dscores = probs * (dprobs - jnp.transpose(delta)[:, :, None])
    probs_low = lax.optimization_barrier(probs.astype(jnp.bfloat16)).astype(jnp.float32)
    dscores_low = lax.optimization_barrier(dscores.astype(jnp.bfloat16)).astype(jnp.float32)
    value_part = jnp.einsum("gqk,qgd->kd", probs_low, grad_f)
    key_part = jnp.einsum("gqk,qgd->kd", dscores_low, query_f) * factor
    query_part = (jnp.einsum("gqk,kd->qgd", dscores_low, key_f) * factor).reshape(L, GROUP * HD)
    return query_part, key_part, value_part


def one_sequence(packed):
    inputs_s, queries_s, keys_s, values_s, outputs_s, grad_s, lse_s, positions_s = packed
    visible = positions_s[None, :] <= positions_s[:, None]
    width = GROUP * HD
    query_list, key_list, value_list, both_list = [], [], [], []
    for head in range(KV_HEADS):
        query_part, key_part, value_part = group_grads(
            queries_s[:, head * width:(head + 1) * width],
            keys_s[:, head * HD:(head + 1) * HD],
            values_s[:, head * HD:(head + 1) * HD],
            grad_s[:, head * width:(head + 1) * width],
            outputs_s[:, head * width:(head + 1) * width],
            lse_s[:, head * GROUP:(head + 1) * GROUP],
            visible)
        query_list.append(query_part)
        key_list.append(key_part)
        value_list.append(value_part)
        both_list.append(key_part)
        both_list.append(value_part)
    kv_low = jnp.concatenate(both_list, axis=1).astype(jnp.bfloat16)
    weight = jnp.dot(jnp.transpose(inputs_s), kv_low, preferred_element_type=jnp.float32)
    return (jnp.concatenate(query_list, axis=1), jnp.concatenate(key_list, axis=1),
            jnp.concatenate(value_list, axis=1), weight)


def reference(inputs, queries, keys, values, outputs, out_grad, lse, positions):
    query_grad, key_grad, value_grad, weights = lax.map(
        one_sequence, (inputs, queries, keys, values, outputs, out_grad, lse, positions))
    return query_grad, key_grad, value_grad, jnp.sum(weights, axis=0)
```

```python
import functools

import jax
import jax.numpy as jnp
from jax import lax
from jax.experimental import pallas as pl
from jax.experimental.pallas import tpu as pltpu
from jax.sharding import PartitionSpec as P

HD = 128
MESH = pl.DeviceIdType.MESH
NT = (((1,), (1,)), ((), ()))
TN = (((0,), (0,)), ((), ()))


def passed_along(block, axis, distance):
    devices = range(lax.axis_size(axis))
    route = [((i - distance) % len(devices), i) for i in devices]
    return lax.ppermute(block, axis, route)


def block_grads(query_blk, grad_blk, lse_blk, delta_blk, query_pos, key_blk, value_blk, key_pos):
    factor = HD ** (-0.5)
    tokens_q = query_blk.shape[0]
    tokens_k = key_blk.shape[0]
    kv_local = key_blk.shape[1] // HD
    group_size = query_blk.shape[1] // key_blk.shape[1]
    query_four = query_blk.reshape(tokens_q, kv_local, group_size, HD)
    grad_four = grad_blk.reshape(tokens_q, kv_local, group_size, HD)
    key_three = key_blk.reshape(tokens_k, kv_local, HD)
    value_three = value_blk.reshape(tokens_k, kv_local, HD)
    lse_four = jnp.transpose(lse_blk.reshape(tokens_q, kv_local, group_size), (1, 2, 0))[..., None]
    delta_four = jnp.transpose(delta_blk.reshape(tokens_q, kv_local, group_size), (1, 2, 0))[
        ..., None
    ]
    visible = key_pos[None, :] <= query_pos[:, None]
    scores = (
        jnp.einsum("qhgd,khd->hgqk", query_four, key_three, preferred_element_type=jnp.float32)
        * factor
    )
    probs = jnp.where(visible, jnp.exp(scores - lse_four), jnp.float32(0.0))
    dprobs = jnp.einsum(
        "qhgd,khd->hgqk", grad_four, value_three, preferred_element_type=jnp.float32
    )
    dscores = probs * (dprobs - delta_four)
    probs_low = probs.astype(jnp.bfloat16)
    dscores_low = dscores.astype(jnp.bfloat16)
    value_part = jnp.einsum(
        "hgqk,qhgd->khd", probs_low, grad_four, preferred_element_type=jnp.float32
    )
    key_part = (
        jnp.einsum("hgqk,qhgd->khd", dscores_low, query_four, preferred_element_type=jnp.float32)
        * factor
    )
    query_part = (
        jnp.einsum("hgqk,khd->qhgd", dscores_low, key_three, preferred_element_type=jnp.float32)
        * factor
    )
    return (
        query_part.reshape(tokens_q, kv_local * group_size * HD),
        key_part.reshape(tokens_k, kv_local * HD),
        value_part.reshape(tokens_k, kv_local * HD),
    )


def shards(inputs, queries, keys, values, outputs, out_grad, lse, positions):
    query_loc = queries[0]
    grad_loc = out_grad[0]
    key_loc = keys[0]
    value_loc = values[0]
    lse_loc = lse[0]
    tokens = query_loc.shape[0]
    heads_q = query_loc.shape[1] // HD
    kv_local = key_loc.shape[1] // HD
    delta_loc = jnp.sum(
        (grad_loc.astype(jnp.float32) * outputs[0].astype(jnp.float32)).reshape(
            tokens, heads_q, HD
        ),
        axis=2,
    )
    pos_loc = positions[0].astype(jnp.float32)
    rounds = lax.axis_size("ctx")
    zero_query = jnp.zeros((tokens, heads_q * HD), jnp.float32)
    zero_key = jnp.zeros((tokens, kv_local * HD), jnp.float32)

    def spin(index, carry):
        key_blk, value_blk, key_acc, value_acc, kpos_blk, dq_acc = carry
        query_part, key_part, value_part = block_grads(
            query_loc, grad_loc, lse_loc, delta_loc, pos_loc, key_blk, value_blk, kpos_blk
        )
        key_blk, value_blk = passed_along((key_blk, value_blk), "ctx", 1)
        key_acc, value_acc, kpos_blk = passed_along(
            (key_acc + key_part, value_acc + value_part, kpos_blk), "ctx", 1
        )
        return (key_blk, value_blk, key_acc, value_acc, kpos_blk, dq_acc + query_part)

    key_blk, value_blk, key_acc, value_acc, kpos_blk, dq_acc = lax.fori_loop(
        0, rounds - 1, spin, (key_loc, value_loc, zero_key, zero_key, pos_loc, zero_query)
    )
    query_part, key_part, value_part = block_grads(
        query_loc, grad_loc, lse_loc, delta_loc, pos_loc, key_blk, value_blk, kpos_blk
    )
    key_grad, value_grad = passed_along((key_acc + key_part, value_acc + value_part), "ctx", 1)
    query_grad = dq_acc + query_part
    kv_low = jnp.stack(
        [key_grad.reshape(tokens, kv_local, HD), value_grad.reshape(tokens, kv_local, HD)], axis=2
    )
    kv_low = kv_low.reshape(tokens, kv_local * 2 * HD).astype(jnp.bfloat16)
    inputs_loc = inputs[0]
    weight_grad = lax.psum_scatter(
        jnp.einsum("td,tc->dc", inputs_loc, kv_low, preferred_element_type=jnp.float32),
        ("dp", "ctx"),
        scatter_dimension=0,
        tiled=True,
    )
    return (query_grad[None], key_grad[None], value_grad[None], weight_grad)


def fused_kernel(
    x_ref, q_ref, k_ref, v_ref, o_ref, g_ref, lse_ref, pos_ref,
    dq_ref, dk_ref, dv_ref, w_ref,
    kv_peer, pos_send, pos_peer, stat, stat_t, part_own, part_send, part_recv, kv_all, x_all,
    local_sem, kv_send, kv_recv, part_ssem, part_rsem,
    xd_send, xd_recv, xx_send, xx_recv, xc_send, xc_recv, g_send, g_recv,
):
    factor = HD ** (-0.5)
    z, h, y = lax.axis_index("dp"), lax.axis_index("heads"), lax.axis_index("ctx")
    me = z * 2 + y
    heads = q_ref.shape[2] // HD
    tokens = q_ref.shape[1]
    half = tokens // 2
    quarter = tokens // 4
    width = w_ref.shape[0]
    core, xpos = h % 2, h // 2
    y_peer = {"ctx": 1 - y}
    x_peer = {"heads": (h + 2) % 4}
    core_peer = {"heads": h + 1 - 2 * core}
    rows_q = pl.ds(pl.multiple_of(half * core + quarter * xpos, quarter), quarter)
    rows_h = pl.ds(pl.multiple_of(half * core, half), half)

    def ring(r):
        other = (me + r) % 8
        return other, {"dp": other // 2, "ctx": other % 2}

    def send(src, dst, ssem, rsem, to):
        return pltpu.make_async_remote_copy(
            src_ref=src, dst_ref=dst, send_sem=ssem, recv_sem=rsem,
            device_id=to, device_id_type=MESH,
        )

    barrier = pltpu.get_barrier_semaphore()
    for r in range(1, 8):
        pl.semaphore_signal(barrier, inc=1, device_id=ring(r)[1], device_id_type=MESH)
    pl.semaphore_signal(barrier, inc=1, device_id=x_peer, device_id_type=MESH)
    pl.semaphore_signal(barrier, inc=1, device_id=core_peer, device_id_type=MESH)
    own_x = pltpu.make_async_copy(
        x_ref.at[0, :, pl.ds(pl.multiple_of(me * width, 128), width)], x_all.at[0], local_sem
    )
    own_x.start()
    pos_send[...] = jnp.broadcast_to(pos_ref[...], pos_send.shape)
    pl.semaphore_wait(barrier, 9)

    kv_copies = [
        send(k_ref.at[0], kv_peer.at[0], kv_send.at[0], kv_recv.at[0], y_peer),
        send(v_ref.at[0], kv_peer.at[1], kv_send.at[1], kv_recv.at[1], y_peer),
        send(pos_send, pos_peer, kv_send.at[2], kv_recv.at[2], y_peer),
    ]
    for copy in kv_copies:
        copy.start()
    direct = {}
    for r in (4, 3, 5, 2, 6, 1, 7):
        other, to = ring(r)
        direct[r] = send(
            x_ref.at[0, rows_q, pl.ds(pl.multiple_of(other * width, 128), width)],
            x_all.at[r, rows_q, :], xd_send.at[r], xd_recv.at[r], to,
        )
        direct[r].start()

    stat[...] = jnp.zeros_like(stat)
    stat[:, 0:heads] = lse_ref[0]
    for i in range(heads):
        cols = slice(i * HD, (i + 1) * HD)
        prod = g_ref[0, :, cols].astype(jnp.float32) * o_ref[0, :, cols].astype(jnp.float32)
        stat[:, heads + i:heads + i + 1] = jnp.sum(prod, axis=1, keepdims=True)
    stat_t[...] = jnp.transpose(stat[...])
    pos_row = pos_ref[...].astype(jnp.float32)

    def column(row):
        return jnp.transpose(jnp.broadcast_to(row, (HD, tokens)))

    def chunk(key, value, key_pos, first, last):
        visible = key_pos <= pos_row

        def one_head(i, carry):
            dk, dv = carry
            cols = pl.ds(pl.multiple_of(i * HD, HD), HD)
            query, grad = q_ref[0, :, cols], g_ref[0, :, cols]
            lse_row = stat_t[pl.ds(i, 1), :]
            delta_row = stat_t[pl.ds(i + heads, 1), :]
            scores = lax.dot_general(key, query, NT, preferred_element_type=jnp.float32) * factor
            probs = jnp.where(visible, jnp.exp(scores - lse_row), jnp.float32(0.0))
            dprobs = lax.dot_general(value, grad, NT, preferred_element_type=jnp.float32)
            dscores = (probs * (dprobs - delta_row)).astype(jnp.bfloat16)
            dv = dv + jnp.dot(probs.astype(jnp.bfloat16), grad, preferred_element_type=jnp.float32)
            dk = dk + jnp.dot(dscores, query, preferred_element_type=jnp.float32)
            dq = lax.dot_general(dscores, key, TN, preferred_element_type=jnp.float32)
            if not first:
                dq = dq_ref[0, :, cols] + dq
            if last:
                dq = dq * factor
            dq_ref[0, :, cols] = dq
            return dk, dv

        zero = jnp.zeros((half, HD), jnp.float32)
        dk, dv = lax.fori_loop(0, heads, one_head, (zero, zero), unroll=2)
        return dk * factor, dv

    def own_chunk(c, first, last):
        rows = slice(c * half, (c + 1) * half)
        dk, dv = chunk(k_ref[0, rows, :], v_ref[0, rows, :], own_col[rows, 0:1], first, last)
        part_own[c, :, 0:HD] = dk
        part_own[c, :, HD:] = dv

    own_col = column(pos_row)
    own_chunk(0, True, False)

    for copy in kv_copies:
        copy.wait_recv()
    peer_col = column(pos_peer[0:1, :].astype(jnp.float32))
    part_copies = []
    for c in range(2):
        rows = slice(c * half, (c + 1) * half)
        dk, dv = chunk(kv_peer[0, rows, :], kv_peer[1, rows, :], peer_col[rows, 0:1], False, False)
        part_send[c, :, 0:HD] = dk.astype(jnp.bfloat16)
        part_send[c, :, HD:] = dv.astype(jnp.bfloat16)
        copy = send(
            part_send.at[c], part_recv.at[c], part_ssem.at[c], part_rsem.at[c], y_peer
        )
        copy.start()
        part_copies.append(copy)
    own_chunk(1, False, True)

    up, down = {"dp": z + 1}, {"dp": z - 1}
    first_z, last_z = 1 - (z + 3) // 4, z // 3

    def pass_block(c, step, r, to_up, to_down):
        rows = slice(c * half, (c + 1) * half)
        src = kv_all.at[r, rows, :]
        slots = ((r + 9 - 2 * y) % 8, (r + 2) % 8, (r + 6) % 8)
        copies = [
            send(src, kv_all.at[slot, rows, :], g_send.at[c, step, d], g_recv.at[c, slot], to)
            for d, (slot, to) in enumerate(zip(slots, (y_peer, up, down)))
        ]
        if to_up is not None:
            pl.when(to_up)(copies[1].start)
            pl.when(to_down)(copies[2].start)
        copies[0].start()
        return copies, to_up, to_down

    passed = []
    for c in range(2):
        rows = slice(c * half, (c + 1) * half)
        part_copies[c].wait_recv()
        total = part_own[c] + part_recv[c].astype(jnp.float32)
        dk_ref[0, rows, :] = total[:, 0:HD]
        dv_ref[0, rows, :] = total[:, HD:]
        kv_all[0, rows, :] = total.astype(jnp.bfloat16)
        passed.append(pass_block(c, 0, 0, z < 3, z > 0))

    def arrived(c, r):
        rows = slice(c * half, (c + 1) * half)
        send(
            kv_all.at[r, rows, :], kv_all.at[r, rows, :], g_send.at[c, 0, 0], g_recv.at[c, r], y_peer
        ).wait_recv()

    def forward_kv(step):
        if step == 1:
            r = 2 + 4 * first_z
        elif step == 2:
            r = 6 - 2 * (first_z + last_z)
        else:
            r = 4 - 2 * first_z + 2 * last_z
        rising = z >= r // 2
        for c in range(2):
            arrived(c, r)
            passed.append(
                pass_block(
                    c, step, r,
                    jnp.logical_and(rising, z < 3),
                    jnp.logical_and(jnp.logical_not(rising), z > 0),
                )
            )

    over_x, over_core = {}, {}

    def forward_x(r):
        direct[r].wait_recv()
        over_x[r] = send(
            x_all.at[r, rows_q, :], x_all.at[r, rows_q, :], xx_send.at[r], xx_recv.at[r], x_peer
        )
        over_x[r].start()

    def forward_core(r):
        over_x[r].wait_recv()
        over_core[r] = send(
            x_all.at[r, rows_h, :], x_all.at[r, rows_h, :], xc_send.at[r], xc_recv.at[r], core_peer
        )
        over_core[r].start()

    def add(r, first=False):
        term = lax.dot_general(x_all[r], kv_all[r], TN, preferred_element_type=jnp.float32)
        w_ref[...] = term if first else w_ref[...] + term

    for r in (1, 7, 2, 6):
        forward_x(r)
    forward_kv(1)
    for r in (3, 5, 4):
        forward_x(r)
    forward_kv(2)
    for r in (1, 7, 2, 6, 3, 5, 4):
        forward_core(r)
    forward_kv(3)
    own_x.wait()
    add(0, True)
    for r in (2, 6, 4):
        over_core[r].wait_recv()
        add(r)
    for r in (1, 7, 3, 5):
        over_core[r].wait_recv()
        arrived(0, r)
        arrived(1, r)
        add(r)

    for copy in kv_copies + part_copies:
        copy.wait_send()
    for r in range(1, 8):
        direct[r].wait_send()
        over_x[r].wait_send()
        over_core[r].wait_send()
    for copies, to_up, to_down in passed:
        copies[0].wait_send()
        pl.when(to_up)(copies[1].wait_send)
        pl.when(to_down)(copies[2].wait_send)


def fused(inputs, queries, keys, values, outputs, out_grad, lse, positions):
    tokens = queries.shape[1]
    width = inputs.shape[2] // 8
    vmem = pl.BlockSpec(memory_space=pltpu.VMEM)
    dma = pltpu.SemaphoreType.DMA
    f32, bf16 = jnp.float32, jnp.bfloat16
    return pl.pallas_call(
        fused_kernel,
        out_shape=(
            jax.ShapeDtypeStruct(queries.shape, f32),
            jax.ShapeDtypeStruct(keys.shape, f32),
            jax.ShapeDtypeStruct(values.shape, f32),
            jax.ShapeDtypeStruct((width, 2 * HD), f32),
        ),
        in_specs=[pl.BlockSpec(memory_space=pl.ANY)] + [vmem] * 7,
        out_specs=(vmem,) * 4,
        scratch_shapes=[
            pltpu.VMEM((2, tokens, HD), bf16),
            pltpu.VMEM((8, tokens), jnp.int32),
            pltpu.VMEM((8, tokens), jnp.int32),
            pltpu.VMEM((tokens, HD), f32),
            pltpu.VMEM((HD, tokens), f32),
            pltpu.VMEM((2, tokens // 2, 2 * HD), f32),
            pltpu.VMEM((2, tokens // 2, 2 * HD), bf16),
            pltpu.VMEM((2, tokens // 2, 2 * HD), bf16),
            pltpu.VMEM((8, tokens, 2 * HD), bf16),
            pltpu.VMEM((8, tokens, width), bf16),
            dma,
            dma((3,)), dma((3,)),
            dma((2,)), dma((2,)),
            dma((8,)), dma((8,)),
            dma((8,)), dma((8,)),
            dma((8,)), dma((8,)),
            dma((2, 4, 3)), dma((2, 8)),
        ],
        compiler_params=pltpu.CompilerParams(
            collective_id=0, has_side_effects=True, vmem_limit_bytes=40 * 1024 * 1024
        ),
    )(inputs, queries, keys, values, outputs, out_grad, lse, positions)


def fits(mesh):
    return mesh.shape["dp"] == 4 and mesh.shape["ctx"] == 2 and mesh.shape["heads"] == 4


def solution(mesh):
    return jax.shard_map(
        fused if fits(mesh) else shards,
        mesh=mesh,
        in_specs=(
            P("dp", "ctx", None),
            P("dp", "ctx", "heads"),
            P("dp", "ctx", "heads"),
            P("dp", "ctx", "heads"),
            P("dp", "ctx", "heads"),
            P("dp", "ctx", "heads"),
            P("dp", "ctx", "heads"),
            P("dp", "ctx"),
        ),
        out_specs=(
            P("dp", "ctx", "heads"),
            P("dp", "ctx", "heads"),
            P("dp", "ctx", "heads"),
            P(("dp", "ctx"), "heads"),
        ),
        check_vma=False,
    )
```

```python
import math

import jax
import jax.numpy as jnp
from jax import lax
from jax.experimental import pallas as pl
from jax.experimental.pallas import tpu as pltpu
from jax.sharding import PartitionSpec as P

HD = 128
MESH = pl.DeviceIdType.MESH
NT = (((1,), (1,)), ((), ()))
TN = (((0,), (0,)), ((), ()))
LOG2E = math.log2(math.e)
VMEM_BYTES = 60 * 1024 * 1024


def passed_along(block, axis, distance):
    devices = range(lax.axis_size(axis))
    route = [((i - distance) % len(devices), i) for i in devices]
    return lax.ppermute(block, axis, route)


def block_grads(query_blk, grad_blk, lse_blk, delta_blk, query_pos, key_blk, value_blk, key_pos):
    factor = HD ** (-0.5)
    tokens_q = query_blk.shape[0]
    tokens_k = key_blk.shape[0]
    kv_local = key_blk.shape[1] // HD
    group_size = query_blk.shape[1] // key_blk.shape[1]
    query_four = query_blk.reshape(tokens_q, kv_local, group_size, HD)
    grad_four = grad_blk.reshape(tokens_q, kv_local, group_size, HD)
    key_three = key_blk.reshape(tokens_k, kv_local, HD)
    value_three = value_blk.reshape(tokens_k, kv_local, HD)
    lse_four = jnp.transpose(lse_blk.reshape(tokens_q, kv_local, group_size), (1, 2, 0))[..., None]
    delta_four = jnp.transpose(delta_blk.reshape(tokens_q, kv_local, group_size), (1, 2, 0))[
        ..., None
    ]
    visible = key_pos[None, :] <= query_pos[:, None]
    scores = (
        jnp.einsum("qhgd,khd->hgqk", query_four, key_three, preferred_element_type=jnp.float32)
        * factor
    )
    probs = jnp.where(visible, jnp.exp(scores - lse_four), jnp.float32(0.0))
    dprobs = jnp.einsum(
        "qhgd,khd->hgqk", grad_four, value_three, preferred_element_type=jnp.float32
    )
    dscores = probs * (dprobs - delta_four)
    probs_low = probs.astype(jnp.bfloat16)
    dscores_low = dscores.astype(jnp.bfloat16)
    value_part = jnp.einsum(
        "hgqk,qhgd->khd", probs_low, grad_four, preferred_element_type=jnp.float32
    )
    key_part = (
        jnp.einsum("hgqk,qhgd->khd", dscores_low, query_four, preferred_element_type=jnp.float32)
        * factor
    )
    query_part = (
        jnp.einsum("hgqk,khd->qhgd", dscores_low, key_three, preferred_element_type=jnp.float32)
        * factor
    )
    return (
        query_part.reshape(tokens_q, kv_local * group_size * HD),
        key_part.reshape(tokens_k, kv_local * HD),
        value_part.reshape(tokens_k, kv_local * HD),
    )


def shards(inputs, queries, keys, values, outputs, out_grad, lse, positions):
    query_loc = queries[0]
    grad_loc = out_grad[0]
    key_loc = keys[0]
    value_loc = values[0]
    lse_loc = lse[0]
    tokens = query_loc.shape[0]
    heads_q = query_loc.shape[1] // HD
    kv_local = key_loc.shape[1] // HD
    delta_loc = jnp.sum(
        (grad_loc.astype(jnp.float32) * outputs[0].astype(jnp.float32)).reshape(
            tokens, heads_q, HD
        ),
        axis=2,
    )
    pos_loc = positions[0].astype(jnp.float32)
    rounds = lax.axis_size("ctx")
    zero_query = jnp.zeros((tokens, heads_q * HD), jnp.float32)
    zero_key = jnp.zeros((tokens, kv_local * HD), jnp.float32)

    def spin(index, carry):
        key_blk, value_blk, key_acc, value_acc, kpos_blk, dq_acc = carry
        query_part, key_part, value_part = block_grads(
            query_loc, grad_loc, lse_loc, delta_loc, pos_loc, key_blk, value_blk, kpos_blk
        )
        key_blk, value_blk = passed_along((key_blk, value_blk), "ctx", 1)
        key_acc, value_acc, kpos_blk = passed_along(
            (key_acc + key_part, value_acc + value_part, kpos_blk), "ctx", 1
        )
        return (key_blk, value_blk, key_acc, value_acc, kpos_blk, dq_acc + query_part)

    key_blk, value_blk, key_acc, value_acc, kpos_blk, dq_acc = lax.fori_loop(
        0, rounds - 1, spin, (key_loc, value_loc, zero_key, zero_key, pos_loc, zero_query)
    )
    query_part, key_part, value_part = block_grads(
        query_loc, grad_loc, lse_loc, delta_loc, pos_loc, key_blk, value_blk, kpos_blk
    )
    key_grad, value_grad = passed_along((key_acc + key_part, value_acc + value_part), "ctx", 1)
    query_grad = dq_acc + query_part
    kv_low = jnp.stack(
        [key_grad.reshape(tokens, kv_local, HD), value_grad.reshape(tokens, kv_local, HD)], axis=2
    )
    kv_low = kv_low.reshape(tokens, kv_local * 2 * HD).astype(jnp.bfloat16)
    inputs_loc = inputs[0]
    weight_grad = lax.psum_scatter(
        jnp.einsum("td,tc->dc", inputs_loc, kv_low, preferred_element_type=jnp.float32),
        ("dp", "ctx"),
        scatter_dimension=0,
        tiled=True,
    )
    return (query_grad[None], key_grad[None], value_grad[None], weight_grad)


def fused_kernel(
    x_ref, q_hbm, k_hbm, v_hbm, o_hbm, g_hbm, lse_hbm, pos_hbm,
    dq_hbm, dk_hbm, dv_hbm, w_hbm,
    dq_ref, dk_ref, dv_ref, w_ref, save_sem,
    q_ref, k_ref, v_ref, o_ref, g_ref, lse_ref, pos_ref, load_sem, kv_peer, pos_send, pos_peer, stat, stat_t, part_own, part_send, part_recv, kv_all, x_all,
    local_sem, kv_send, kv_recv, part_ssem, part_rsem,
    xd_send, xd_recv, xx_send, xx_recv, xc_send, xc_recv, g_send, g_recv,
):
    factor = HD ** (-0.5)
    z, h, y = lax.axis_index("dp"), lax.axis_index("heads"), lax.axis_index("ctx")
    me = z * 2 + y
    heads = q_ref.shape[2] // HD
    tokens = q_ref.shape[1]
    half = tokens // 2
    quarter = tokens // 4
    width = w_ref.shape[0]
    core, xpos = h % 2, h // 2
    y_peer = {"ctx": 1 - y}
    x_peer = {"heads": (h + 2) % 4}
    core_peer = {"heads": h + 1 - 2 * core}
    rows_q = pl.ds(pl.multiple_of(half * core + quarter * xpos, quarter), quarter)
    rows_h = pl.ds(pl.multiple_of(half * core, half), half)

    def ring(r):
        other = (me + r) % 8
        return other, {"dp": other // 2, "ctx": other % 2}

    def send(src, dst, ssem, rsem, to):
        return pltpu.make_async_remote_copy(
            src_ref=src, dst_ref=dst, send_sem=ssem, recv_sem=rsem,
            device_id=to, device_id_type=MESH,
        )

    loads = [
        pltpu.make_async_copy(src, dst, load_sem.at[i])
        for i, (src, dst) in enumerate((
            (pos_hbm, pos_ref), (k_hbm, k_ref), (v_hbm, v_ref), (lse_hbm, lse_ref),
            (g_hbm, g_ref), (o_hbm, o_ref), (q_hbm, q_ref),
        ))
    ]
    for copy in loads:
        copy.start()
    barrier = pltpu.get_barrier_semaphore()
    for r in range(1, 8):
        pl.semaphore_signal(barrier, inc=1, device_id=ring(r)[1], device_id_type=MESH)
    pl.semaphore_signal(barrier, inc=1, device_id=x_peer, device_id_type=MESH)
    pl.semaphore_signal(barrier, inc=1, device_id=core_peer, device_id_type=MESH)
    own_x = pltpu.make_async_copy(
        x_ref.at[0, :, pl.ds(pl.multiple_of(me * width, 128), width)], x_all.at[0], local_sem
    )
    own_x.start()
    for copy in loads[:3]:
        copy.wait()
    pos_send[...] = jnp.broadcast_to(pos_ref[...], pos_send.shape)
    pl.semaphore_wait(barrier, 9)

    kv_copies = [
        send(k_ref.at[0], kv_peer.at[0], kv_send.at[0], kv_recv.at[0], y_peer),
        send(v_ref.at[0], kv_peer.at[1], kv_send.at[1], kv_recv.at[1], y_peer),
        send(pos_send, pos_peer, kv_send.at[2], kv_recv.at[2], y_peer),
    ]
    for copy in kv_copies:
        copy.start()
    direct = {}

    def send_x(r):
        other, to = ring(r)
        direct[r] = send(
            x_ref.at[0, rows_q, pl.ds(pl.multiple_of(other * width, 128), width)],
            x_all.at[r, rows_q, :], xd_send.at[r], xd_recv.at[r], to,
        )
        direct[r].start()

    for r in (4, 2, 6):
        send_x(r)

    for copy in loads[3:]:
        copy.wait()
    stat[...] = jnp.zeros_like(stat)
    for i in range(heads):
        cols = slice(i * HD, (i + 1) * HD)
        prod = g_ref[0, :, cols].astype(jnp.float32) * o_ref[0, :, cols].astype(jnp.float32)
        stat[:, i:i + 1] = jnp.sum(prod, axis=1, keepdims=True)
    stat_t[...] = jnp.transpose(stat[...])
    lse_low = lse_ref[0] * LOG2E
    pos_row = pos_ref[...].astype(jnp.float32)

    def column(row):
        return jnp.transpose(jnp.broadcast_to(row, (HD, tokens)))

    def chunk(key, value, key_pos, first, last):
        visible = key_pos <= pos_row

        dk = jnp.zeros((half, HD), jnp.float32)
        dv = jnp.zeros((half, HD), jnp.float32)
        for i in range(heads):
            cols = slice(i * HD, (i + 1) * HD)
            query, grad = q_ref[0, :, cols], g_ref[0, :, cols]
            scores = lax.dot_general(key, query, NT, preferred_element_type=jnp.float32)
            probs = jnp.exp2(scores * (factor * LOG2E) - lse_low[i:i + 1, :])
            probs = jnp.where(visible, probs, jnp.float32(0.0))
            dprobs = lax.dot_general(value, grad, NT, preferred_element_type=jnp.float32)
            dscores = (probs * (dprobs - stat_t[i:i + 1, :])).astype(jnp.bfloat16)
            dv = dv + jnp.dot(probs.astype(jnp.bfloat16), grad, preferred_element_type=jnp.float32)
            dk = dk + jnp.dot(dscores, query, preferred_element_type=jnp.float32)
            dq = lax.dot_general(dscores, key, TN, preferred_element_type=jnp.float32)
            if not first:
                dq = dq_ref[0, :, cols] + dq
            if last:
                dq = dq * factor
            dq_ref[0, :, cols] = dq
        return dk * factor, dv

    def own_chunk(c, first, last):
        rows = slice(c * half, (c + 1) * half)
        dk, dv = chunk(k_ref[0, rows, :], v_ref[0, rows, :], own_col[rows, 0:1], first, last)
        part_own[c, :, 0:HD] = dk
        part_own[c, :, HD:] = dv

    over_x, over_core = {}, {}

    def forward_x(r):
        direct[r].wait_recv()
        over_x[r] = send(
            x_all.at[r, rows_q, :], x_all.at[r, rows_q, :], xx_send.at[r], xx_recv.at[r], x_peer
        )
        over_x[r].start()

    def forward_core(r):
        over_x[r].wait_recv()
        over_core[r] = send(
            x_all.at[r, rows_h, :], x_all.at[r, rows_h, :], xc_send.at[r], xc_recv.at[r], core_peer
        )
        over_core[r].start()

    own_col = column(pos_row)
    own_chunk(0, True, False)
    for r in (3, 5, 1, 7):
        send_x(r)

    for copy in kv_copies:
        copy.wait_recv()
    peer_col = column(pos_peer[0:1, :].astype(jnp.float32))
    part_copies = []
    for c in range(2):
        rows = slice(c * half, (c + 1) * half)
        dk, dv = chunk(kv_peer[0, rows, :], kv_peer[1, rows, :], peer_col[rows, 0:1], False, False)
        part_send[c, :, 0:HD] = dk.astype(jnp.bfloat16)
        part_send[c, :, HD:] = dv.astype(jnp.bfloat16)
        copy = send(
            part_send.at[c], part_recv.at[c], part_ssem.at[c], part_rsem.at[c], y_peer
        )
        copy.start()
        part_copies.append(copy)
    for r in (2, 6, 4):
        forward_x(r)
    own_chunk(1, False, True)
    saves = [
        pltpu.make_async_copy(src, dst, save_sem.at[i])
        for i, (src, dst) in enumerate((
            (dq_ref, dq_hbm), (dk_ref, dk_hbm), (dv_ref, dv_hbm), (w_ref, w_hbm),
        ))
    ]
    saves[0].start()

    up, down = {"dp": z + 1}, {"dp": z - 1}
    first_z, last_z = 1 - (z + 3) // 4, z // 3

    def pass_block(c, step, r, to_up, to_down):
        rows = slice(c * half, (c + 1) * half)
        src = kv_all.at[r, rows, :]
        slots = ((r + 9 - 2 * y) % 8, (r + 2) % 8, (r + 6) % 8)
        copies = [
            send(src, kv_all.at[slot, rows, :], g_send.at[c, step, d], g_recv.at[c, slot], to)
            for d, (slot, to) in enumerate(zip(slots, (y_peer, up, down)))
        ]
        if to_up is not None:
            pl.when(to_up)(copies[1].start)
            pl.when(to_down)(copies[2].start)
        copies[0].start()
        return copies, to_up, to_down

    passed = []
    for c in range(2):
        rows = slice(c * half, (c + 1) * half)
        part_copies[c].wait_recv()
        total = part_own[c] + part_recv[c].astype(jnp.float32)
        dk_ref[0, rows, :] = total[:, 0:HD]
        dv_ref[0, rows, :] = total[:, HD:]
        kv_all[0, rows, :] = total.astype(jnp.bfloat16)
        passed.append(pass_block(c, 0, 0, z < 3, z > 0))

    def arrived(c, r):
        rows = slice(c * half, (c + 1) * half)
        send(
            kv_all.at[r, rows, :], kv_all.at[r, rows, :], g_send.at[c, 0, 0], g_recv.at[c, r], y_peer
        ).wait_recv()

    def forward_kv(step):
        if step == 1:
            r = 2 + 4 * first_z
        elif step == 2:
            r = 6 - 2 * (first_z + last_z)
        else:
            r = 4 - 2 * first_z + 2 * last_z
        rising = z >= r // 2
        for c in range(2):
            arrived(c, r)
            passed.append(
                pass_block(
                    c, step, r,
                    jnp.logical_and(rising, z < 3),
                    jnp.logical_and(jnp.logical_not(rising), z > 0),
                )
            )

    def add(r, first=False):
        term = lax.dot_general(x_all[r], kv_all[r], TN, preferred_element_type=jnp.float32)
        w_ref[...] = term if first else w_ref[...] + term

    saves[1].start()
    saves[2].start()
    own_x.wait()
    add(0, True)
    forward_kv(1)
    for r in (2, 6, 4):
        forward_core(r)
    for r in (1, 7, 3, 5):
        forward_x(r)
    forward_kv(2)
    forward_kv(3)
    for r in (2, 6, 4):
        over_core[r].wait_recv()
        add(r)
    for r in (1, 7, 3, 5):
        forward_core(r)
    for r in (1, 7, 3, 5):
        over_core[r].wait_recv()
        arrived(0, r)
        arrived(1, r)
        add(r)

    saves[3].start()
    for copy in kv_copies + part_copies:
        copy.wait_send()
    for r in range(1, 8):
        direct[r].wait_send()
        over_x[r].wait_send()
        over_core[r].wait_send()
    for copies, to_up, to_down in passed:
        copies[0].wait_send()
        pl.when(to_up)(copies[1].wait_send)
        pl.when(to_down)(copies[2].wait_send)
    for copy in saves:
        copy.wait()


def write_kernel(*refs):
    sources, results, sem = refs[:4], refs[4:8], refs[8]
    copies = [
        pltpu.make_async_copy(src, dst, sem.at[i])
        for i, (src, dst) in enumerate(zip(sources, results))
    ]
    for copy in copies:
        copy.start()
    for copy in copies:
        copy.wait()


def fused(inputs, queries, keys, values, outputs, out_grad, lse, positions):
    tokens = queries.shape[1]
    width = inputs.shape[2] // 8
    hbm = pl.BlockSpec(memory_space=pltpu.HBM)
    dma = pltpu.SemaphoreType.DMA
    f32, bf16 = jnp.float32, jnp.bfloat16
    lse_rows = jnp.transpose(lse, (0, 2, 1))
    args = (inputs, queries, keys, values, outputs, out_grad, lse_rows, positions)
    shapes = (
        jax.ShapeDtypeStruct(queries.shape, f32),
        jax.ShapeDtypeStruct(keys.shape, f32),
        jax.ShapeDtypeStruct(values.shape, f32),
        jax.ShapeDtypeStruct((width, 2 * HD), f32),
    )
    grads = pl.pallas_call(
        fused_kernel,
        out_shape=shapes,
        in_specs=[hbm] * 8,
        out_specs=(hbm,) * 4,
        scratch_shapes=[pltpu.VMEM(a.shape, a.dtype) for a in shapes] + [
            dma((4,)),
        ] + [pltpu.VMEM(a.shape, a.dtype) for a in args[1:]] + [
            dma((7,)),
            pltpu.VMEM((2, tokens, HD), bf16),
            pltpu.VMEM((8, tokens), jnp.int32),
            pltpu.VMEM((8, tokens), jnp.int32),
            pltpu.VMEM((tokens, HD), f32),
            pltpu.VMEM((HD, tokens), f32),
            pltpu.VMEM((2, tokens // 2, 2 * HD), f32),
            pltpu.VMEM((2, tokens // 2, 2 * HD), bf16),
            pltpu.VMEM((2, tokens // 2, 2 * HD), bf16),
            pltpu.VMEM((8, tokens, 2 * HD), bf16),
            pltpu.VMEM((8, tokens, width), bf16),
            dma,
            dma((3,)), dma((3,)),
            dma((2,)), dma((2,)),
            dma((8,)), dma((8,)),
            dma((8,)), dma((8,)),
            dma((8,)), dma((8,)),
            dma((2, 4, 3)), dma((2, 8)),
        ],
        compiler_params=pltpu.CompilerParams(
            collective_id=0, has_side_effects=True, vmem_limit_bytes=VMEM_BYTES
        ),
    )(*args)
    return pl.pallas_call(
        write_kernel,
        out_shape=shapes,
        in_specs=[hbm] * 4,
        out_specs=(hbm,) * 4,
        scratch_shapes=[dma((4,))],
        compiler_params=pltpu.CompilerParams(vmem_limit_bytes=VMEM_BYTES),
    )(*grads)


def fits(mesh):
    return mesh.shape["dp"] == 4 and mesh.shape["ctx"] == 2 and mesh.shape["heads"] == 4


def solution(mesh):
    return jax.shard_map(
        fused if fits(mesh) else shards,
        mesh=mesh,
        in_specs=(
            P("dp", "ctx", None),
            P("dp", "ctx", "heads"),
            P("dp", "ctx", "heads"),
            P("dp", "ctx", "heads"),
            P("dp", "ctx", "heads"),
            P("dp", "ctx", "heads"),
            P("dp", "ctx", "heads"),
            P("dp", "ctx"),
        ),
        out_specs=(
            P("dp", "ctx", "heads"),
            P("dp", "ctx", "heads"),
            P("dp", "ctx", "heads"),
            P(("dp", "ctx"), "heads"),
        ),
        check_vma=False,
    )
```

```python
import math

import jax
import jax.numpy as jnp
from jax import lax
from jax.experimental import pallas as pl
from jax.experimental.pallas import tpu as pltpu
from jax.sharding import PartitionSpec as P

HD = 128
MESH = pl.DeviceIdType.MESH
NT = (((1,), (1,)), ((), ()))
TN = (((0,), (0,)), ((), ()))
LOG2E = math.log2(math.e)
VMEM_BYTES = 60 * 1024 * 1024


def passed_along(block, axis, distance):
    devices = range(lax.axis_size(axis))
    route = [((i - distance) % len(devices), i) for i in devices]
    return lax.ppermute(block, axis, route)


def block_grads(query_blk, grad_blk, lse_blk, delta_blk, query_pos, key_blk, value_blk, key_pos):
    factor = HD ** (-0.5)
    tokens_q = query_blk.shape[0]
    tokens_k = key_blk.shape[0]
    kv_local = key_blk.shape[1] // HD
    group_size = query_blk.shape[1] // key_blk.shape[1]
    query_four = query_blk.reshape(tokens_q, kv_local, group_size, HD)
    grad_four = grad_blk.reshape(tokens_q, kv_local, group_size, HD)
    key_three = key_blk.reshape(tokens_k, kv_local, HD)
    value_three = value_blk.reshape(tokens_k, kv_local, HD)
    lse_four = jnp.transpose(lse_blk.reshape(tokens_q, kv_local, group_size), (1, 2, 0))[..., None]
    delta_four = jnp.transpose(delta_blk.reshape(tokens_q, kv_local, group_size), (1, 2, 0))[
        ..., None
    ]
    visible = key_pos[None, :] <= query_pos[:, None]
    scores = (
        jnp.einsum("qhgd,khd->hgqk", query_four, key_three, preferred_element_type=jnp.float32)
        * factor
    )
    probs = jnp.where(visible, jnp.exp(scores - lse_four), jnp.float32(0.0))
    dprobs = jnp.einsum(
        "qhgd,khd->hgqk", grad_four, value_three, preferred_element_type=jnp.float32
    )
    dscores = probs * (dprobs - delta_four)
    probs_low = probs.astype(jnp.bfloat16)
    dscores_low = dscores.astype(jnp.bfloat16)
    value_part = jnp.einsum(
        "hgqk,qhgd->khd", probs_low, grad_four, preferred_element_type=jnp.float32
    )
    key_part = (
        jnp.einsum("hgqk,qhgd->khd", dscores_low, query_four, preferred_element_type=jnp.float32)
        * factor
    )
    query_part = (
        jnp.einsum("hgqk,khd->qhgd", dscores_low, key_three, preferred_element_type=jnp.float32)
        * factor
    )
    return (
        query_part.reshape(tokens_q, kv_local * group_size * HD),
        key_part.reshape(tokens_k, kv_local * HD),
        value_part.reshape(tokens_k, kv_local * HD),
    )


def shards(inputs, queries, keys, values, outputs, out_grad, lse, positions):
    query_loc = queries[0]
    grad_loc = out_grad[0]
    key_loc = keys[0]
    value_loc = values[0]
    lse_loc = lse[0]
    tokens = query_loc.shape[0]
    heads_q = query_loc.shape[1] // HD
    kv_local = key_loc.shape[1] // HD
    delta_loc = jnp.sum(
        (grad_loc.astype(jnp.float32) * outputs[0].astype(jnp.float32)).reshape(
            tokens, heads_q, HD
        ),
        axis=2,
    )
    pos_loc = positions[0].astype(jnp.float32)
    rounds = lax.axis_size("ctx")
    zero_query = jnp.zeros((tokens, heads_q * HD), jnp.float32)
    zero_key = jnp.zeros((tokens, kv_local * HD), jnp.float32)

    def spin(index, carry):
        key_blk, value_blk, key_acc, value_acc, kpos_blk, dq_acc = carry
        query_part, key_part, value_part = block_grads(
            query_loc, grad_loc, lse_loc, delta_loc, pos_loc, key_blk, value_blk, kpos_blk
        )
        key_blk, value_blk = passed_along((key_blk, value_blk), "ctx", 1)
        key_acc, value_acc, kpos_blk = passed_along(
            (key_acc + key_part, value_acc + value_part, kpos_blk), "ctx", 1
        )
        return (key_blk, value_blk, key_acc, value_acc, kpos_blk, dq_acc + query_part)

    key_blk, value_blk, key_acc, value_acc, kpos_blk, dq_acc = lax.fori_loop(
        0, rounds - 1, spin, (key_loc, value_loc, zero_key, zero_key, pos_loc, zero_query)
    )
    query_part, key_part, value_part = block_grads(
        query_loc, grad_loc, lse_loc, delta_loc, pos_loc, key_blk, value_blk, kpos_blk
    )
    key_grad, value_grad = passed_along((key_acc + key_part, value_acc + value_part), "ctx", 1)
    query_grad = dq_acc + query_part
    kv_low = jnp.stack(
        [key_grad.reshape(tokens, kv_local, HD), value_grad.reshape(tokens, kv_local, HD)], axis=2
    )
    kv_low = kv_low.reshape(tokens, kv_local * 2 * HD).astype(jnp.bfloat16)
    inputs_loc = inputs[0]
    weight_grad = lax.psum_scatter(
        jnp.einsum("td,tc->dc", inputs_loc, kv_low, preferred_element_type=jnp.float32),
        ("dp", "ctx"),
        scatter_dimension=0,
        tiled=True,
    )
    return (query_grad[None], key_grad[None], value_grad[None], weight_grad)


def fused_kernel(
    x_ref, q_hbm, k_hbm, v_hbm, o_hbm, g_hbm, lse_hbm, pos_hbm,
    dq_hbm, dk_hbm, dv_hbm, w_hbm,
    dq_ref, dk_ref, dv_ref, w_ref, save_sem,
    q_ref, k_ref, v_ref, o_ref, g_ref, lse_ref, pos_ref, load_sem,
    kv_peer, pos_send, pos_peer, qt_ref, gt_ref, dqt_ref, xt_all, part_send, part_recv, kv_all, x_all,
    local_sem, kv_send, kv_recv, part_ssem, part_rsem,
    xd_send, xd_recv, xx_send, xx_recv, xc_send, xc_recv, g_send, g_recv,
):
    factor = HD ** (-0.5)
    z, h, y = lax.axis_index("dp"), lax.axis_index("heads"), lax.axis_index("ctx")
    me = z * 2 + y
    heads = q_ref.shape[2] // HD
    tokens = q_ref.shape[1]
    half = tokens // 2
    quarter = tokens // 4
    width = w_ref.shape[0]
    core, xpos = h % 2, h // 2
    y_peer = {"ctx": 1 - y}
    x_peer = {"heads": (h + 2) % 4}
    core_peer = {"heads": h + 1 - 2 * core}
    rows_q = pl.ds(pl.multiple_of(half * core + quarter * xpos, quarter), quarter)
    rows_h = pl.ds(pl.multiple_of(half * core, half), half)

    def ring(r):
        other = (me + r) % 8
        return other, {"dp": other // 2, "ctx": other % 2}

    def send(src, dst, ssem, rsem, to):
        return pltpu.make_async_remote_copy(
            src_ref=src, dst_ref=dst, send_sem=ssem, recv_sem=rsem,
            device_id=to, device_id_type=MESH,
        )

    loads = [
        pltpu.make_async_copy(src, dst, load_sem.at[i])
        for i, (src, dst) in enumerate((
            (pos_hbm, pos_ref), (k_hbm, k_ref), (v_hbm, v_ref), (lse_hbm, lse_ref),
            (g_hbm, g_ref), (o_hbm, o_ref), (q_hbm, q_ref),
        ))
    ]
    for copy in loads:
        copy.start()
    barrier = pltpu.get_barrier_semaphore()
    for r in range(1, 8):
        pl.semaphore_signal(barrier, inc=1, device_id=ring(r)[1], device_id_type=MESH)
    pl.semaphore_signal(barrier, inc=1, device_id=x_peer, device_id_type=MESH)
    pl.semaphore_signal(barrier, inc=1, device_id=core_peer, device_id_type=MESH)
    own_x = pltpu.make_async_copy(
        x_ref.at[0, :, pl.ds(pl.multiple_of(me * width, 128), width)], x_all.at[0], local_sem
    )
    own_x.start()
    for copy in loads[:3]:
        copy.wait()
    pos_send[...] = jnp.broadcast_to(pos_ref[...], pos_send.shape)
    pl.semaphore_wait(barrier, 9)

    kv_copies = [
        send(k_ref.at[0], kv_peer.at[0], kv_send.at[0], kv_recv.at[0], y_peer),
        send(v_ref.at[0], kv_peer.at[1], kv_send.at[1], kv_recv.at[1], y_peer),
        send(pos_send, pos_peer, kv_send.at[2], kv_recv.at[2], y_peer),
    ]
    for copy in kv_copies:
        copy.start()
    direct = {}

    def send_x(r):
        other, to = ring(r)
        direct[r] = send(
            x_ref.at[0, rows_q, pl.ds(pl.multiple_of(other * width, 128), width)],
            x_all.at[r, rows_q, :], xd_send.at[r], xd_recv.at[r], to,
        )
        direct[r].start()

    for r in (4, 2, 6):
        send_x(r)

    for copy in loads[3:]:
        copy.wait()
    ones = jnp.ones((8, HD), jnp.bfloat16)
    delta = []
    for i in range(heads):
        cols = slice(i * HD, (i + 1) * HD)
        qt_ref[i] = jnp.transpose(q_ref[0, :, cols])
        gt_ref[i] = jnp.transpose(g_ref[0, :, cols])
        prod = g_ref[0, :, cols].astype(jnp.float32) * o_ref[0, :, cols].astype(jnp.float32)
        high = prod.astype(jnp.bfloat16)
        low = (prod - high.astype(jnp.float32)).astype(jnp.bfloat16)
        both = lax.dot_general(ones, high, NT, preferred_element_type=jnp.float32)
        both = both + lax.dot_general(ones, low, NT, preferred_element_type=jnp.float32)
        delta.append(both[0:1, :])
    lse_low = lse_ref[0] * LOG2E
    pos_row = pos_ref[...].astype(jnp.float32)

    def column(row):
        return jnp.transpose(jnp.broadcast_to(row, (HD, tokens)))

    def block(key, value, key_pos, first):
        visible = key_pos <= pos_row
        key_t = jnp.transpose(key)
        dk = jnp.zeros((tokens, HD), jnp.float32)
        dv = jnp.zeros((tokens, HD), jnp.float32)
        for i in range(heads):
            cols = slice(i * HD, (i + 1) * HD)
            scores = jnp.dot(key, qt_ref[i], preferred_element_type=jnp.float32)
            probs = jnp.exp2(scores * (factor * LOG2E) - lse_low[i:i + 1, :])
            probs = jnp.where(visible, probs, jnp.float32(0.0))
            dprobs = jnp.dot(value, gt_ref[i], preferred_element_type=jnp.float32)
            dscores = (probs * (dprobs - delta[i])).astype(jnp.bfloat16)
            probs = probs.astype(jnp.bfloat16)
            dv = dv + jnp.dot(probs, g_ref[0, :, cols], preferred_element_type=jnp.float32)
            dk = dk + jnp.dot(dscores, q_ref[0, :, cols], preferred_element_type=jnp.float32)
            dqt = jnp.dot(key_t, dscores, preferred_element_type=jnp.float32)
            if first:
                dqt_ref[i] = dqt
            else:
                dq_ref[0, :, cols] = jnp.transpose((dqt_ref[i] + dqt) * factor)
        return dk * factor, dv

    over_x, over_core = {}, {}

    def forward_x(r):
        direct[r].wait_recv()
        over_x[r] = send(
            x_all.at[r, rows_q, :], x_all.at[r, rows_q, :], xx_send.at[r], xx_recv.at[r], x_peer
        )
        over_x[r].start()

    def forward_core(r):
        over_x[r].wait_recv()
        over_core[r] = send(
            x_all.at[r, rows_h, :], x_all.at[r, rows_h, :], xc_send.at[r], xc_recv.at[r], core_peer
        )
        over_core[r].start()

    for copy in kv_copies:
        copy.wait_recv()
    for r in (3, 5, 1, 7):
        send_x(r)
    dk, dv = block(
        kv_peer[0], kv_peer[1], column(pos_peer[0:1, :].astype(jnp.float32))[:, 0:1], True
    )
    part_copies = []
    for c in range(2):
        rows = slice(c * half, (c + 1) * half)
        part_send[c, :, 0:HD] = dk[rows].astype(jnp.bfloat16)
        part_send[c, :, HD:] = dv[rows].astype(jnp.bfloat16)
        copy = send(
            part_send.at[c], part_recv.at[c], part_ssem.at[c], part_rsem.at[c], y_peer
        )
        copy.start()
        part_copies.append(copy)
    for r in (2, 6, 4):
        forward_x(r)
    dk_own, dv_own = block(k_ref[0], v_ref[0], column(pos_row)[:, 0:1], False)
    saves = [
        pltpu.make_async_copy(src, dst, save_sem.at[i])
        for i, (src, dst) in enumerate((
            (dq_ref, dq_hbm), (dk_ref, dk_hbm), (dv_ref, dv_hbm), (w_ref, w_hbm),
        ))
    ]
    saves[0].start()

    up, down = {"dp": z + 1}, {"dp": z - 1}
    first_z, last_z = 1 - (z + 3) // 4, z // 3

    def pass_block(c, step, r, to_up, to_down):
        rows = slice(c * half, (c + 1) * half)
        src = kv_all.at[r, rows, :]
        slots = ((r + 9 - 2 * y) % 8, (r + 2) % 8, (r + 6) % 8)
        copies = [
            send(src, kv_all.at[slot, rows, :], g_send.at[c, step, d], g_recv.at[c, slot], to)
            for d, (slot, to) in enumerate(zip(slots, (y_peer, up, down)))
        ]
        if to_up is not None:
            pl.when(to_up)(copies[1].start)
            pl.when(to_down)(copies[2].start)
        copies[0].start()
        return copies, to_up, to_down

    passed = []
    for c in range(2):
        rows = slice(c * half, (c + 1) * half)
        part_copies[c].wait_recv()
        dk = dk_own[rows] + part_recv[c, :, 0:HD].astype(jnp.float32)
        dv = dv_own[rows] + part_recv[c, :, HD:].astype(jnp.float32)
        dk_ref[0, rows, :] = dk
        dv_ref[0, rows, :] = dv
        kv_all[0, rows, 0:HD] = dk.astype(jnp.bfloat16)
        kv_all[0, rows, HD:] = dv.astype(jnp.bfloat16)
        passed.append(pass_block(c, 0, 0, z < 3, z > 0))

    def arrived(c, r):
        rows = slice(c * half, (c + 1) * half)
        send(
            kv_all.at[r, rows, :], kv_all.at[r, rows, :], g_send.at[c, 0, 0], g_recv.at[c, r], y_peer
        ).wait_recv()

    turns = (
        2 + 4 * first_z, 6 - 2 * (first_z + last_z), 4 - 2 * first_z + 2 * last_z
    )
    odd_turns = [(r + 7 + 2 * y) % 8 for r in (0,) + turns]

    def forward_kv(step):
        r = turns[step - 1]
        rising = z >= r // 2
        for c in range(2):
            arrived(c, r)
            passed.append(
                pass_block(
                    c, step, r,
                    jnp.logical_and(rising, z < 3),
                    jnp.logical_and(jnp.logical_not(rising), z > 0),
                )
            )

    def turn_x(r):
        xt_all[r] = jnp.transpose(x_all[r])

    def add(r, first=False):
        term = jnp.dot(xt_all[r], kv_all[r], preferred_element_type=jnp.float32)
        w_ref[...] = term if first else w_ref[...] + term

    saves[1].start()
    saves[2].start()
    for r in (2, 6, 4):
        forward_core(r)
    own_x.wait()
    turn_x(0)
    add(0, True)
    forward_kv(1)
    for r in (1, 7, 3, 5):
        forward_x(r)
    for r in (2, 6, 4):
        over_core[r].wait_recv()
        turn_x(r)
    forward_kv(2)
    add(turns[0])
    add(turns[1])
    forward_kv(3)
    for r in (1, 7, 3, 5):
        forward_core(r)
    add(turns[2])
    for r in (1, 7, 3, 5):
        over_core[r].wait_recv()
        turn_x(r)
    for r in odd_turns:
        arrived(0, r)
        arrived(1, r)
        add(r)
    saves[3].start()
    for copy in kv_copies + part_copies:
        copy.wait_send()
    for r in range(1, 8):
        direct[r].wait_send()
        over_x[r].wait_send()
        over_core[r].wait_send()
    for copies, to_up, to_down in passed:
        copies[0].wait_send()
        pl.when(to_up)(copies[1].wait_send)
        pl.when(to_down)(copies[2].wait_send)
    for copy in saves:
        copy.wait()


def write_kernel(*refs):
    sources, results, held, sem_in, sem_out = refs[:4], refs[4:8], refs[8:12], refs[12], refs[13]
    whole = [(i, slice(None)) for i in range(1, 4)]
    quarter = held[0].shape[1] // 4
    parts = whole + [(0, slice(c * quarter, (c + 1) * quarter)) for c in range(4)]
    copies = []
    for n, (i, rows) in enumerate(parts):
        at = (0, rows) if i == 0 else (slice(None),)
        copies.append((
            pltpu.make_async_copy(sources[i].at[at], held[i].at[at], sem_in.at[n]),
            pltpu.make_async_copy(held[i].at[at], results[i].at[at], sem_out.at[n]),
        ))
    for into, _ in copies:
        into.start()
    for into, out in copies:
        into.wait()
        out.start()
    for _, out in copies:
        out.wait()


def fused(inputs, queries, keys, values, outputs, out_grad, lse, positions):
    tokens = queries.shape[1]
    width = inputs.shape[2] // 8
    hbm = pl.BlockSpec(memory_space=pltpu.HBM)
    dma = pltpu.SemaphoreType.DMA
    f32, bf16 = jnp.float32, jnp.bfloat16
    lse_rows = jnp.transpose(lse, (0, 2, 1))
    args = (inputs, queries, keys, values, outputs, out_grad, lse_rows, positions)
    shapes = (
        jax.ShapeDtypeStruct(queries.shape, f32),
        jax.ShapeDtypeStruct(keys.shape, f32),
        jax.ShapeDtypeStruct(values.shape, f32),
        jax.ShapeDtypeStruct((width, 2 * HD), f32),
    )
    grads = pl.pallas_call(
        fused_kernel,
        out_shape=shapes,
        in_specs=[hbm] * 8,
        out_specs=(hbm,) * 4,
        scratch_shapes=[pltpu.VMEM(a.shape, a.dtype) for a in shapes] + [
            dma((4,)),
        ] + [pltpu.VMEM(a.shape, a.dtype) for a in args[1:]] + [
            dma((7,)),
            pltpu.VMEM((2, tokens, HD), bf16),
            pltpu.VMEM((8, tokens), jnp.int32),
            pltpu.VMEM((8, tokens), jnp.int32),
            pltpu.VMEM((queries.shape[2] // HD, HD, tokens), bf16),
            pltpu.VMEM((queries.shape[2] // HD, HD, tokens), bf16),
            pltpu.VMEM((queries.shape[2] // HD, HD, tokens), f32),
            pltpu.VMEM((8, width, tokens), bf16),
            pltpu.VMEM((2, tokens // 2, 2 * HD), bf16),
            pltpu.VMEM((2, tokens // 2, 2 * HD), bf16),
            pltpu.VMEM((8, tokens, 2 * HD), bf16),
            pltpu.VMEM((8, tokens, width), bf16),
            dma,
            dma((3,)), dma((3,)),
            dma((2,)), dma((2,)),
            dma((8,)), dma((8,)),
            dma((8,)), dma((8,)),
            dma((8,)), dma((8,)),
            dma((2, 4, 3)), dma((2, 8)),
        ],
        compiler_params=pltpu.CompilerParams(
            collective_id=0, has_side_effects=True, vmem_limit_bytes=VMEM_BYTES
        ),
    )(*args)
    return pl.pallas_call(
        write_kernel,
        out_shape=shapes,
        in_specs=[hbm] * 4,
        out_specs=(hbm,) * 4,
        scratch_shapes=[pltpu.VMEM(a.shape, a.dtype) for a in shapes] + [dma((7,)), dma((7,))],
        compiler_params=pltpu.CompilerParams(vmem_limit_bytes=VMEM_BYTES),
    )(*grads)


def fits(mesh):
    return mesh.shape["dp"] == 4 and mesh.shape["ctx"] == 2 and mesh.shape["heads"] == 4


def solution(mesh):
    return jax.shard_map(
        fused if fits(mesh) else shards,
        mesh=mesh,
        in_specs=(
            P("dp", "ctx", None),
            P("dp", "ctx", "heads"),
            P("dp", "ctx", "heads"),
            P("dp", "ctx", "heads"),
            P("dp", "ctx", "heads"),
            P("dp", "ctx", "heads"),
            P("dp", "ctx", "heads"),
            P("dp", "ctx"),
        ),
        out_specs=(
            P("dp", "ctx", "heads"),
            P("dp", "ctx", "heads"),
            P("dp", "ctx", "heads"),
            P(("dp", "ctx"), "heads"),
        ),
        check_vma=False,
    )
```

```python
import math

import jax
import jax.numpy as jnp
from jax import lax
from jax.experimental import pallas as pl
from jax.experimental.pallas import tpu as pltpu
from jax.sharding import PartitionSpec as P

HD = 128
MESH = pl.DeviceIdType.MESH
NT = (((1,), (1,)), ((), ()))
TN = (((0,), (0,)), ((), ()))
LOG2E = math.log2(math.e)
VMEM_BYTES = 60 * 1024 * 1024


def passed_along(block, axis, distance):
    devices = range(lax.axis_size(axis))
    route = [((i - distance) % len(devices), i) for i in devices]
    return lax.ppermute(block, axis, route)


def block_grads(query_blk, grad_blk, lse_blk, delta_blk, query_pos, key_blk, value_blk, key_pos):
    factor = HD ** (-0.5)
    tokens_q = query_blk.shape[0]
    tokens_k = key_blk.shape[0]
    kv_local = key_blk.shape[1] // HD
    group_size = query_blk.shape[1] // key_blk.shape[1]
    query_four = query_blk.reshape(tokens_q, kv_local, group_size, HD)
    grad_four = grad_blk.reshape(tokens_q, kv_local, group_size, HD)
    key_three = key_blk.reshape(tokens_k, kv_local, HD)
    value_three = value_blk.reshape(tokens_k, kv_local, HD)
    lse_four = jnp.transpose(lse_blk.reshape(tokens_q, kv_local, group_size), (1, 2, 0))[..., None]
    delta_four = jnp.transpose(delta_blk.reshape(tokens_q, kv_local, group_size), (1, 2, 0))[
        ..., None
    ]
    visible = key_pos[None, :] <= query_pos[:, None]
    scores = (
        jnp.einsum("qhgd,khd->hgqk", query_four, key_three, preferred_element_type=jnp.float32)
        * factor
    )
    probs = jnp.where(visible, jnp.exp(scores - lse_four), jnp.float32(0.0))
    dprobs = jnp.einsum(
        "qhgd,khd->hgqk", grad_four, value_three, preferred_element_type=jnp.float32
    )
    dscores = probs * (dprobs - delta_four)
    probs_low = probs.astype(jnp.bfloat16)
    dscores_low = dscores.astype(jnp.bfloat16)
    value_part = jnp.einsum(
        "hgqk,qhgd->khd", probs_low, grad_four, preferred_element_type=jnp.float32
    )
    key_part = (
        jnp.einsum("hgqk,qhgd->khd", dscores_low, query_four, preferred_element_type=jnp.float32)
        * factor
    )
    query_part = (
        jnp.einsum("hgqk,khd->qhgd", dscores_low, key_three, preferred_element_type=jnp.float32)
        * factor
    )
    return (
        query_part.reshape(tokens_q, kv_local * group_size * HD),
        key_part.reshape(tokens_k, kv_local * HD),
        value_part.reshape(tokens_k, kv_local * HD),
    )


def shards(inputs, queries, keys, values, outputs, out_grad, lse, positions):
    query_loc = queries[0]
    grad_loc = out_grad[0]
    key_loc = keys[0]
    value_loc = values[0]
    lse_loc = lse[0]
    tokens = query_loc.shape[0]
    heads_q = query_loc.shape[1] // HD
    kv_local = key_loc.shape[1] // HD
    delta_loc = jnp.sum(
        (grad_loc.astype(jnp.float32) * outputs[0].astype(jnp.float32)).reshape(
            tokens, heads_q, HD
        ),
        axis=2,
    )
    pos_loc = positions[0].astype(jnp.float32)
    rounds = lax.axis_size("ctx")
    zero_query = jnp.zeros((tokens, heads_q * HD), jnp.float32)
    zero_key = jnp.zeros((tokens, kv_local * HD), jnp.float32)

    def spin(index, carry):
        key_blk, value_blk, key_acc, value_acc, kpos_blk, dq_acc = carry
        query_part, key_part, value_part = block_grads(
            query_loc, grad_loc, lse_loc, delta_loc, pos_loc, key_blk, value_blk, kpos_blk
        )
        key_blk, value_blk = passed_along((key_blk, value_blk), "ctx", 1)
        key_acc, value_acc, kpos_blk = passed_along(
            (key_acc + key_part, value_acc + value_part, kpos_blk), "ctx", 1
        )
        return (key_blk, value_blk, key_acc, value_acc, kpos_blk, dq_acc + query_part)

    key_blk, value_blk, key_acc, value_acc, kpos_blk, dq_acc = lax.fori_loop(
        0, rounds - 1, spin, (key_loc, value_loc, zero_key, zero_key, pos_loc, zero_query)
    )
    query_part, key_part, value_part = block_grads(
        query_loc, grad_loc, lse_loc, delta_loc, pos_loc, key_blk, value_blk, kpos_blk
    )
    key_grad, value_grad = passed_along((key_acc + key_part, value_acc + value_part), "ctx", 1)
    query_grad = dq_acc + query_part
    kv_low = jnp.stack(
        [key_grad.reshape(tokens, kv_local, HD), value_grad.reshape(tokens, kv_local, HD)], axis=2
    )
    kv_low = kv_low.reshape(tokens, kv_local * 2 * HD).astype(jnp.bfloat16)
    inputs_loc = inputs[0]
    weight_grad = lax.psum_scatter(
        jnp.einsum("td,tc->dc", inputs_loc, kv_low, preferred_element_type=jnp.float32),
        ("dp", "ctx"),
        scatter_dimension=0,
        tiled=True,
    )
    return (query_grad[None], key_grad[None], value_grad[None], weight_grad)


def fused_kernel(
    x_ref, q_hbm, k_hbm, v_hbm, o_hbm, g_hbm, lse_hbm, pos_hbm,
    dq_hbm, dk_hbm, dv_hbm, w_hbm,
    dq_ref, dk_ref, dv_ref, w_ref, save_sem,
    q_ref, k_ref, v_ref, o_ref, g_ref, lse_ref, pos_ref, load_sem,
    kv_peer, pos_send, pos_peer, qt_ref, gt_ref, dqt_ref, xt_all, part_send, part_recv, kv_all, x_all,
    local_sem, kv_send, kv_recv, part_ssem, part_rsem,
    xd_send, xd_recv, xx_send, xx_recv, xc_send, xc_recv, g_send, g_recv,
):
    factor = HD ** (-0.5)
    z, h, y = lax.axis_index("dp"), lax.axis_index("heads"), lax.axis_index("ctx")
    me = z * 2 + y
    heads = q_ref.shape[2] // HD
    tokens = q_ref.shape[1]
    half = tokens // 2
    quarter = tokens // 4
    width = w_ref.shape[0]
    core, xpos = h % 2, h // 2
    y_peer = {"ctx": 1 - y}
    x_peer = {"heads": (h + 2) % 4}
    core_peer = {"heads": h + 1 - 2 * core}
    rows_q = pl.ds(pl.multiple_of(half * core + quarter * xpos, quarter), quarter)
    rows_h = pl.ds(pl.multiple_of(half * core, half), half)

    def ring(r):
        other = (me + r) % 8
        return other, {"dp": other // 2, "ctx": other % 2}

    def send(src, dst, ssem, rsem, to):
        return pltpu.make_async_remote_copy(
            src_ref=src, dst_ref=dst, send_sem=ssem, recv_sem=rsem,
            device_id=to, device_id_type=MESH,
        )

    loads = [
        pltpu.make_async_copy(src, dst, load_sem.at[i])
        for i, (src, dst) in enumerate((
            (pos_hbm, pos_ref), (k_hbm, k_ref), (v_hbm, v_ref), (lse_hbm, lse_ref),
            (g_hbm, g_ref), (o_hbm, o_ref), (q_hbm, q_ref),
        ))
    ]
    for copy in loads:
        copy.start()
    barrier = pltpu.get_barrier_semaphore()
    for r in range(1, 8):
        pl.semaphore_signal(barrier, inc=1, device_id=ring(r)[1], device_id_type=MESH)
    pl.semaphore_signal(barrier, inc=1, device_id=x_peer, device_id_type=MESH)
    pl.semaphore_signal(barrier, inc=1, device_id=core_peer, device_id_type=MESH)
    own_x = pltpu.make_async_copy(
        x_ref.at[0, :, pl.ds(pl.multiple_of(me * width, 128), width)], x_all.at[0], local_sem
    )
    own_x.start()
    for copy in loads[:3]:
        copy.wait()
    pos_send[...] = jnp.broadcast_to(pos_ref[...], pos_send.shape)
    pl.semaphore_wait(barrier, 9)

    kv_copies = [
        send(k_ref.at[0], kv_peer.at[0], kv_send.at[0], kv_recv.at[0], y_peer),
        send(v_ref.at[0], kv_peer.at[1], kv_send.at[1], kv_recv.at[1], y_peer),
        send(pos_send, pos_peer, kv_send.at[2], kv_recv.at[2], y_peer),
    ]
    for copy in kv_copies:
        copy.start()
    first_z, last_z = 1 - (z + 3) // 4, z // 3
    turns = (2 + 4 * first_z, 6 - 2 * (first_z + last_z), 4 - 2 * first_z + 2 * last_z)
    odd_turns = [(r + 7 + 2 * y) % 8 for r in (0,) + turns]
    order = [r for pair in zip(odd_turns, turns) for r in pair] + odd_turns[3:]

    def direct(r, other, to):
        return send(
            x_ref.at[0, rows_q, pl.ds(pl.multiple_of(other * width, 128), width)],
            x_all.at[r, rows_q, :], xd_send.at[r], xd_recv.at[r], to,
        )

    for r in order:
        back = (8 - r) % 8
        direct(back, *ring(back)).start()

    for copy in loads[3:]:
        copy.wait()
    ones = jnp.ones((8, HD), jnp.bfloat16)
    delta = []
    for i in range(heads):
        cols = slice(i * HD, (i + 1) * HD)
        qt_ref[i] = jnp.transpose(q_ref[0, :, cols])
        gt_ref[i] = jnp.transpose(g_ref[0, :, cols])
        prod = g_ref[0, :, cols].astype(jnp.float32) * o_ref[0, :, cols].astype(jnp.float32)
        high = prod.astype(jnp.bfloat16)
        low = (prod - high.astype(jnp.float32)).astype(jnp.bfloat16)
        both = lax.dot_general(ones, high, NT, preferred_element_type=jnp.float32)
        both = both + lax.dot_general(ones, low, NT, preferred_element_type=jnp.float32)
        delta.append(both[0:1, :])
    lse_low = lse_ref[0] * LOG2E
    pos_row = pos_ref[...].astype(jnp.float32)

    def column(row):
        return jnp.transpose(jnp.broadcast_to(row, (HD, tokens)))

    def block(key, value, key_pos, first, forwards):
        visible = key_pos <= pos_row
        key_t = jnp.transpose(key)
        dk = jnp.zeros((tokens, HD), jnp.float32)
        dv = jnp.zeros((tokens, HD), jnp.float32)
        for i in range(heads):
            cols = slice(i * HD, (i + 1) * HD)
            scores = jnp.dot(key, qt_ref[i], preferred_element_type=jnp.float32)
            probs = jnp.exp2(scores * (factor * LOG2E) - lse_low[i:i + 1, :])
            probs = jnp.where(visible, probs, jnp.float32(0.0))
            dprobs = jnp.dot(value, gt_ref[i], preferred_element_type=jnp.float32)
            dscores = (probs * (dprobs - delta[i])).astype(jnp.bfloat16)
            probs = probs.astype(jnp.bfloat16)
            dv = dv + jnp.dot(probs, g_ref[0, :, cols], preferred_element_type=jnp.float32)
            dk = dk + jnp.dot(dscores, q_ref[0, :, cols], preferred_element_type=jnp.float32)
            dqt = jnp.dot(key_t, dscores, preferred_element_type=jnp.float32)
            if first:
                dqt_ref[i] = dqt
            else:
                dq_ref[0, :, cols] = jnp.transpose((dqt_ref[i] + dqt) * factor)
            if i in forwards:
                forward_x(forwards[i])
        return dk * factor, dv

    def over_x(r):
        part = x_all.at[r, rows_q, :]
        return send(part, part, xx_send.at[r], xx_recv.at[r], x_peer)

    def over_core(r):
        part = x_all.at[r, rows_h, :]
        return send(part, part, xc_send.at[r], xc_recv.at[r], core_peer)

    def forward_x(n):
        direct(order[n], *ring(order[n])).wait_recv()
        over_x(order[n]).start()

    def forward_core(n):
        over_x(order[n]).wait_recv()
        over_core(order[n]).start()

    for copy in kv_copies:
        copy.wait_recv()
    dk, dv = block(
        kv_peer[0], kv_peer[1], column(pos_peer[0:1, :].astype(jnp.float32))[:, 0:1], True, {}
    )
    part_copies = []
    for c in range(2):
        rows = slice(c * half, (c + 1) * half)
        part_send[c, :, 0:HD] = dk[rows].astype(jnp.bfloat16)
        part_send[c, :, HD:] = dv[rows].astype(jnp.bfloat16)
        copy = send(
            part_send.at[c], part_recv.at[c], part_ssem.at[c], part_rsem.at[c], y_peer
        )
        copy.start()
        part_copies.append(copy)
    dk_own, dv_own = block(
        k_ref[0], v_ref[0], column(pos_row)[:, 0:1], False, {0: 0, 2: 1, 4: 2, 6: 3}
    )
    saves = [
        pltpu.make_async_copy(src, dst, save_sem.at[i])
        for i, (src, dst) in enumerate((
            (dq_ref, dq_hbm), (dk_ref, dk_hbm), (dv_ref, dv_hbm), (w_ref, w_hbm),
        ))
    ]
    saves[0].start()

    up, down = {"dp": z + 1}, {"dp": z - 1}

    def pass_block(c, step, r, to_up, to_down):
        rows = slice(c * half, (c + 1) * half)
        src = kv_all.at[r, rows, :]
        slots = ((r + 9 - 2 * y) % 8, (r + 2) % 8, (r + 6) % 8)
        copies = [
            send(src, kv_all.at[slot, rows, :], g_send.at[c, step, d], g_recv.at[c, slot], to)
            for d, (slot, to) in enumerate(zip(slots, (y_peer, up, down)))
        ]
        if to_up is not None:
            pl.when(to_up)(copies[1].start)
            pl.when(to_down)(copies[2].start)
        copies[0].start()
        return copies, to_up, to_down

    passed = []
    for c in range(2):
        rows = slice(c * half, (c + 1) * half)
        part_copies[c].wait_recv()
        dk = dk_own[rows] + part_recv[c, :, 0:HD].astype(jnp.float32)
        dv = dv_own[rows] + part_recv[c, :, HD:].astype(jnp.float32)
        dk_ref[0, rows, :] = dk
        dv_ref[0, rows, :] = dv
        kv_all[0, rows, 0:HD] = dk.astype(jnp.bfloat16)
        kv_all[0, rows, HD:] = dv.astype(jnp.bfloat16)
        passed.append(pass_block(c, 0, 0, z < 3, z > 0))

    def arrived(c, r):
        rows = slice(c * half, (c + 1) * half)
        send(
            kv_all.at[r, rows, :], kv_all.at[r, rows, :], g_send.at[c, 0, 0], g_recv.at[c, r], y_peer
        ).wait_recv()

    def forward_kv(step):
        r = turns[step - 1]
        rising = z >= r // 2
        for c in range(2):
            arrived(c, r)
            passed.append(
                pass_block(
                    c, step, r,
                    jnp.logical_and(rising, z < 3),
                    jnp.logical_and(jnp.logical_not(rising), z > 0),
                )
            )

    def turn_x(n):
        over_core(order[n]).wait_recv()
        xt_all[order[n]] = jnp.transpose(x_all[order[n]])

    def add(r):
        w_ref[...] += jnp.dot(xt_all[r], kv_all[r], preferred_element_type=jnp.float32)

    def add_odd(n):
        arrived(0, odd_turns[n])
        arrived(1, odd_turns[n])
        add(odd_turns[n])

    saves[1].start()
    saves[2].start()
    forward_x(4)
    for n in (0, 1, 2):
        forward_core(n)
    own_x.wait()
    xt_all[0] = jnp.transpose(x_all[0])
    w_ref[...] = jnp.dot(xt_all[0], kv_all[0], preferred_element_type=jnp.float32)
    forward_kv(1)
    forward_x(5)
    forward_x(6)
    forward_core(3)
    forward_core(4)
    for n in (0, 1, 2):
        turn_x(n)
    forward_kv(2)
    add(turns[0])
    add_odd(0)
    turn_x(3)
    forward_core(5)
    add(turns[1])
    turn_x(4)
    forward_kv(3)
    forward_core(6)
    add_odd(1)
    turn_x(5)
    add(turns[2])
    add_odd(2)
    turn_x(6)
    add_odd(3)

    saves[3].start()
    for copy in kv_copies + part_copies:
        copy.wait_send()
    for r in range(1, 8):
        direct(r, *ring(r)).wait_send()
        over_x(r).wait_send()
        over_core(r).wait_send()
    for copies, to_up, to_down in passed:
        copies[0].wait_send()
        pl.when(to_up)(copies[1].wait_send)
        pl.when(to_down)(copies[2].wait_send)
    for copy in saves:
        copy.wait()


def write_kernel(*refs):
    sources, results, held, sem_in, sem_out = refs[:4], refs[4:8], refs[8:12], refs[12], refs[13]
    whole = [(i, slice(None)) for i in range(1, 4)]
    quarter = held[0].shape[1] // 4
    parts = whole + [(0, slice(c * quarter, (c + 1) * quarter)) for c in range(4)]
    copies = []
    for n, (i, rows) in enumerate(parts):
        at = (0, rows) if i == 0 else (slice(None),)
        copies.append((
            pltpu.make_async_copy(sources[i].at[at], held[i].at[at], sem_in.at[n]),
            pltpu.make_async_copy(held[i].at[at], results[i].at[at], sem_out.at[n]),
        ))
    for into, _ in copies:
        into.start()
    for into, out in copies:
        into.wait()
        out.start()
    for _, out in copies:
        out.wait()


def fused(inputs, queries, keys, values, outputs, out_grad, lse, positions):
    tokens = queries.shape[1]
    width = inputs.shape[2] // 8
    hbm = pl.BlockSpec(memory_space=pltpu.HBM)
    dma = pltpu.SemaphoreType.DMA
    f32, bf16 = jnp.float32, jnp.bfloat16
    lse_rows = jnp.transpose(lse, (0, 2, 1))
    args = (inputs, queries, keys, values, outputs, out_grad, lse_rows, positions)
    shapes = (
        jax.ShapeDtypeStruct(queries.shape, f32),
        jax.ShapeDtypeStruct(keys.shape, f32),
        jax.ShapeDtypeStruct(values.shape, f32),
        jax.ShapeDtypeStruct((width, 2 * HD), f32),
    )
    grads = pl.pallas_call(
        fused_kernel,
        out_shape=shapes,
        in_specs=[hbm] * 8,
        out_specs=(hbm,) * 4,
        scratch_shapes=[pltpu.VMEM(a.shape, a.dtype) for a in shapes] + [
            dma((4,)),
        ] + [pltpu.VMEM(a.shape, a.dtype) for a in args[1:]] + [
            dma((7,)),
            pltpu.VMEM((2, tokens, HD), bf16),
            pltpu.VMEM((8, tokens), jnp.int32),
            pltpu.VMEM((8, tokens), jnp.int32),
            pltpu.VMEM((queries.shape[2] // HD, HD, tokens), bf16),
            pltpu.VMEM((queries.shape[2] // HD, HD, tokens), bf16),
            pltpu.VMEM((queries.shape[2] // HD, HD, tokens), f32),
            pltpu.VMEM((8, width, tokens), bf16),
            pltpu.VMEM((2, tokens // 2, 2 * HD), bf16),
            pltpu.VMEM((2, tokens // 2, 2 * HD), bf16),
            pltpu.VMEM((8, tokens, 2 * HD), bf16),
            pltpu.VMEM((8, tokens, width), bf16),
            dma,
            dma((3,)), dma((3,)),
            dma((2,)), dma((2,)),
            dma((8,)), dma((8,)),
            dma((8,)), dma((8,)),
            dma((8,)), dma((8,)),
            dma((2, 4, 3)), dma((2, 8)),
        ],
        compiler_params=pltpu.CompilerParams(
            collective_id=0, has_side_effects=True, vmem_limit_bytes=VMEM_BYTES
        ),
    )(*args)
    return pl.pallas_call(
        write_kernel,
        out_shape=shapes,
        in_specs=[hbm] * 4,
        out_specs=(hbm,) * 4,
        scratch_shapes=[pltpu.VMEM(a.shape, a.dtype) for a in shapes] + [dma((7,)), dma((7,))],
        compiler_params=pltpu.CompilerParams(vmem_limit_bytes=VMEM_BYTES),
    )(*grads)


def fits(mesh):
    return mesh.shape["dp"] == 4 and mesh.shape["ctx"] == 2 and mesh.shape["heads"] == 4


def solution(mesh):
    return jax.shard_map(
        fused if fits(mesh) else shards,
        mesh=mesh,
        in_specs=(
            P("dp", "ctx", None),
            P("dp", "ctx", "heads"),
            P("dp", "ctx", "heads"),
            P("dp", "ctx", "heads"),
            P("dp", "ctx", "heads"),
            P("dp", "ctx", "heads"),
            P("dp", "ctx", "heads"),
            P("dp", "ctx"),
        ),
        out_specs=(
            P("dp", "ctx", "heads"),
            P("dp", "ctx", "heads"),
            P("dp", "ctx", "heads"),
            P(("dp", "ctx"), "heads"),
        ),
        check_vma=False,
    )
```

```python
import math

import jax
import jax.numpy as jnp
from jax import lax
from jax.experimental import pallas as pl
from jax.experimental.pallas import tpu as pltpu
from jax.sharding import PartitionSpec as P

HD = 128
MESH = pl.DeviceIdType.MESH
NT = (((1,), (1,)), ((), ()))
TN = (((0,), (0,)), ((), ()))
LOG2E = math.log2(math.e)
VMEM_BYTES = 60 * 1024 * 1024


def passed_along(block, axis, distance):
    devices = range(lax.axis_size(axis))
    route = [((i - distance) % len(devices), i) for i in devices]
    return lax.ppermute(block, axis, route)


def block_grads(query_blk, grad_blk, lse_blk, delta_blk, query_pos, key_blk, value_blk, key_pos):
    factor = HD ** (-0.5)
    tokens_q = query_blk.shape[0]
    tokens_k = key_blk.shape[0]
    kv_local = key_blk.shape[1] // HD
    group_size = query_blk.shape[1] // key_blk.shape[1]
    query_four = query_blk.reshape(tokens_q, kv_local, group_size, HD)
    grad_four = grad_blk.reshape(tokens_q, kv_local, group_size, HD)
    key_three = key_blk.reshape(tokens_k, kv_local, HD)
    value_three = value_blk.reshape(tokens_k, kv_local, HD)
    lse_four = jnp.transpose(lse_blk.reshape(tokens_q, kv_local, group_size), (1, 2, 0))[..., None]
    delta_four = jnp.transpose(delta_blk.reshape(tokens_q, kv_local, group_size), (1, 2, 0))[
        ..., None
    ]
    visible = key_pos[None, :] <= query_pos[:, None]
    scores = (
        jnp.einsum("qhgd,khd->hgqk", query_four, key_three, preferred_element_type=jnp.float32)
        * factor
    )
    probs = jnp.where(visible, jnp.exp(scores - lse_four), jnp.float32(0.0))
    dprobs = jnp.einsum(
        "qhgd,khd->hgqk", grad_four, value_three, preferred_element_type=jnp.float32
    )
    dscores = probs * (dprobs - delta_four)
    probs_low = probs.astype(jnp.bfloat16)
    dscores_low = dscores.astype(jnp.bfloat16)
    value_part = jnp.einsum(
        "hgqk,qhgd->khd", probs_low, grad_four, preferred_element_type=jnp.float32
    )
    key_part = (
        jnp.einsum("hgqk,qhgd->khd", dscores_low, query_four, preferred_element_type=jnp.float32)
        * factor
    )
    query_part = (
        jnp.einsum("hgqk,khd->qhgd", dscores_low, key_three, preferred_element_type=jnp.float32)
        * factor
    )
    return (
        query_part.reshape(tokens_q, kv_local * group_size * HD),
        key_part.reshape(tokens_k, kv_local * HD),
        value_part.reshape(tokens_k, kv_local * HD),
    )


def shards(inputs, queries, keys, values, outputs, out_grad, lse, positions):
    query_loc = queries[0]
    grad_loc = out_grad[0]
    key_loc = keys[0]
    value_loc = values[0]
    lse_loc = lse[0]
    tokens = query_loc.shape[0]
    heads_q = query_loc.shape[1] // HD
    kv_local = key_loc.shape[1] // HD
    delta_loc = jnp.sum(
        (grad_loc.astype(jnp.float32) * outputs[0].astype(jnp.float32)).reshape(
            tokens, heads_q, HD
        ),
        axis=2,
    )
    pos_loc = positions[0].astype(jnp.float32)
    rounds = lax.axis_size("ctx")
    zero_query = jnp.zeros((tokens, heads_q * HD), jnp.float32)
    zero_key = jnp.zeros((tokens, kv_local * HD), jnp.float32)

    def spin(index, carry):
        key_blk, value_blk, key_acc, value_acc, kpos_blk, dq_acc = carry
        query_part, key_part, value_part = block_grads(
            query_loc, grad_loc, lse_loc, delta_loc, pos_loc, key_blk, value_blk, kpos_blk
        )
        key_blk, value_blk = passed_along((key_blk, value_blk), "ctx", 1)
        key_acc, value_acc, kpos_blk = passed_along(
            (key_acc + key_part, value_acc + value_part, kpos_blk), "ctx", 1
        )
        return (key_blk, value_blk, key_acc, value_acc, kpos_blk, dq_acc + query_part)

    key_blk, value_blk, key_acc, value_acc, kpos_blk, dq_acc = lax.fori_loop(
        0, rounds - 1, spin, (key_loc, value_loc, zero_key, zero_key, pos_loc, zero_query)
    )
    query_part, key_part, value_part = block_grads(
        query_loc, grad_loc, lse_loc, delta_loc, pos_loc, key_blk, value_blk, kpos_blk
    )
    key_grad, value_grad = passed_along((key_acc + key_part, value_acc + value_part), "ctx", 1)
    query_grad = dq_acc + query_part
    kv_low = jnp.stack(
        [key_grad.reshape(tokens, kv_local, HD), value_grad.reshape(tokens, kv_local, HD)], axis=2
    )
    kv_low = kv_low.reshape(tokens, kv_local * 2 * HD).astype(jnp.bfloat16)
    inputs_loc = inputs[0]
    weight_grad = lax.psum_scatter(
        jnp.einsum("td,tc->dc", inputs_loc, kv_low, preferred_element_type=jnp.float32),
        ("dp", "ctx"),
        scatter_dimension=0,
        tiled=True,
    )
    return (query_grad[None], key_grad[None], value_grad[None], weight_grad)


def fused_kernel(
    x_ref, q_hbm, k_hbm, v_hbm, o_hbm, g_hbm, lse_hbm, pos_hbm,
    dq_hbm, dk_hbm, dv_hbm, w_hbm,
    dq_ref, dk_ref, dv_ref, w_ref, save_sem,
    q_ref, k_ref, v_ref, o_ref, g_ref, lse_ref, pos_ref, load_sem,
    kv_peer, pos_send, pos_peer, qt_ref, gt_ref, dqt_ref, xt_all, part_send, part_recv, kv_all, x_all,
    local_sem, kv_send, kv_recv, part_ssem, part_rsem,
    xd_send, xd_recv, xx_send, xx_recv, xc_send, xc_recv, g_send, g_recv,
):
    factor = HD ** (-0.5)
    z, h, y = lax.axis_index("dp"), lax.axis_index("heads"), lax.axis_index("ctx")
    me = z * 2 + y
    heads = q_ref.shape[2] // HD
    tokens = q_ref.shape[1]
    half = tokens // 2
    quarter = tokens // 4
    width = w_ref.shape[0]
    core, xpos = h % 2, h // 2
    y_peer = {"ctx": 1 - y}
    x_peer = {"heads": (h + 2) % 4}
    core_peer = {"heads": h + 1 - 2 * core}
    rows_q = pl.ds(pl.multiple_of(half * core + quarter * xpos, quarter), quarter)
    rows_h = pl.ds(pl.multiple_of(half * core, half), half)

    def ring(r):
        other = (me + r) % 8
        return other, {"dp": other // 2, "ctx": other % 2}

    def send(src, dst, ssem, rsem, to):
        return pltpu.make_async_remote_copy(
            src_ref=src, dst_ref=dst, send_sem=ssem, recv_sem=rsem,
            device_id=to, device_id_type=MESH,
        )

    loads = [
        pltpu.make_async_copy(src, dst, load_sem.at[i])
        for i, (src, dst) in enumerate((
            (pos_hbm, pos_ref), (k_hbm, k_ref), (v_hbm, v_ref), (lse_hbm, lse_ref),
            (g_hbm, g_ref), (o_hbm, o_ref), (q_hbm, q_ref),
        ))
    ]
    for copy in loads:
        copy.start()
    barrier = pltpu.get_barrier_semaphore()
    for r in range(1, 8):
        pl.semaphore_signal(barrier, inc=1, device_id=ring(r)[1], device_id_type=MESH)
    pl.semaphore_signal(barrier, inc=1, device_id=x_peer, device_id_type=MESH)
    pl.semaphore_signal(barrier, inc=1, device_id=core_peer, device_id_type=MESH)
    own_x = pltpu.make_async_copy(
        x_ref.at[0, :, pl.ds(pl.multiple_of(me * width, 128), width)], x_all.at[0], local_sem
    )
    own_x.start()
    for copy in loads[:3]:
        copy.wait()
    pos_send[...] = jnp.broadcast_to(pos_ref[...], pos_send.shape)
    pl.semaphore_wait(barrier, 9)

    kv_copies = [
        send(k_ref.at[0], kv_peer.at[0], kv_send.at[0], kv_recv.at[0], y_peer),
        send(v_ref.at[0], kv_peer.at[1], kv_send.at[1], kv_recv.at[1], y_peer),
        send(pos_send, pos_peer, kv_send.at[2], kv_recv.at[2], y_peer),
    ]
    for copy in kv_copies:
        copy.start()
    first_z, last_z = 1 - (z + 3) // 4, z // 3
    turns = (2 + 4 * first_z, 6 - 2 * (first_z + last_z), 4 - 2 * first_z + 2 * last_z)
    odd_turns = [(r + 7 + 2 * y) % 8 for r in (0,) + turns]
    order = [r for pair in zip(odd_turns, turns) for r in pair] + odd_turns[3:]

    def direct(r, other, to):
        return send(
            x_ref.at[0, rows_q, pl.ds(pl.multiple_of(other * width, 128), width)],
            x_all.at[r, rows_q, :], xd_send.at[r], xd_recv.at[r], to,
        )

    def send_x(slots):
        for r in slots:
            back = (8 - r) % 8
            direct(back, *ring(back)).start()

    send_x(turns)

    for copy in loads[3:]:
        copy.wait()
    ones = jnp.ones((8, HD), jnp.bfloat16)
    delta = []
    for i in range(heads):
        cols = slice(i * HD, (i + 1) * HD)
        qt_ref[i] = jnp.transpose(q_ref[0, :, cols])
        gt_ref[i] = jnp.transpose(g_ref[0, :, cols])
        prod = g_ref[0, :, cols].astype(jnp.float32) * o_ref[0, :, cols].astype(jnp.float32)
        high = prod.astype(jnp.bfloat16)
        low = (prod - high.astype(jnp.float32)).astype(jnp.bfloat16)
        both = lax.dot_general(ones, high, NT, preferred_element_type=jnp.float32)
        both = both + lax.dot_general(ones, low, NT, preferred_element_type=jnp.float32)
        delta.append(both[0:1, :])
    lse_low = lse_ref[0] * LOG2E
    pos_row = pos_ref[...].astype(jnp.float32)

    def column(row):
        return jnp.transpose(jnp.broadcast_to(row, (HD, tokens)))

    def block(key, value, visible, which, sums, seen):
        key_t = jnp.transpose(key)
        dk, dv = sums
        for i in which:
            cols = slice(i * HD, (i + 1) * HD)
            scores = jnp.dot(key, qt_ref[i], preferred_element_type=jnp.float32)
            probs = jnp.exp2(scores * (factor * LOG2E) - lse_low[i:i + 1, :])
            probs = jnp.where(visible, probs, jnp.float32(0.0))
            dprobs = jnp.dot(value, gt_ref[i], preferred_element_type=jnp.float32)
            dscores = (probs * (dprobs - delta[i])).astype(jnp.bfloat16)
            probs = probs.astype(jnp.bfloat16)
            dv = dv + jnp.dot(probs, g_ref[0, :, cols], preferred_element_type=jnp.float32)
            dk = dk + jnp.dot(dscores, q_ref[0, :, cols], preferred_element_type=jnp.float32)
            dqt = jnp.dot(key_t, dscores, preferred_element_type=jnp.float32)
            if i in seen:
                dq_ref[0, :, cols] = jnp.transpose((dqt_ref[i] + dqt) * factor)
            else:
                dqt_ref[i] = dqt
        return dk, dv

    def over_x(r):
        part = x_all.at[r, rows_q, :]
        return send(part, part, xx_send.at[r], xx_recv.at[r], x_peer)

    def over_core(r):
        part = x_all.at[r, rows_h, :]
        return send(part, part, xc_send.at[r], xc_recv.at[r], core_peer)

    def forward_x(n):
        direct(order[n], *ring(order[n])).wait_recv()
        over_x(order[n]).start()

    def forward_core(n):
        over_x(order[n]).wait_recv()
        over_core(order[n]).start()

    zero = jnp.zeros((tokens, HD), jnp.float32)
    early, late = range(heads // 2), range(heads // 2, heads)
    own_sees = column(pos_row)[:, 0:1] <= pos_row
    own_sums = block(k_ref[0], v_ref[0], own_sees, early, (zero, zero), ())
    for copy in kv_copies:
        copy.wait_recv()
    send_x(odd_turns)
    peer_sees = column(pos_peer[0:1, :].astype(jnp.float32))[:, 0:1] <= pos_row
    dk, dv = block(kv_peer[0], kv_peer[1], peer_sees, range(heads), (zero, zero), early)
    dk = dk * factor
    part_copies = []
    for c in range(2):
        rows = slice(c * half, (c + 1) * half)
        part_send[c, :, 0:HD] = dk[rows].astype(jnp.bfloat16)
        part_send[c, :, HD:] = dv[rows].astype(jnp.bfloat16)
        copy = send(
            part_send.at[c], part_recv.at[c], part_ssem.at[c], part_rsem.at[c], y_peer
        )
        copy.start()
        part_copies.append(copy)
    dk_own, dv_own = block(k_ref[0], v_ref[0], own_sees, late, own_sums, late)
    dk_own = dk_own * factor
    saves = [
        pltpu.make_async_copy(src, dst, save_sem.at[i])
        for i, (src, dst) in enumerate((
            (dq_ref, dq_hbm), (dk_ref, dk_hbm), (dv_ref, dv_hbm), (w_ref, w_hbm),
        ))
    ]
    saves[0].start()

    up, down = {"dp": z + 1}, {"dp": z - 1}

    def pass_block(c, step, r, to_up, to_down):
        rows = slice(c * quarter, (c + 1) * quarter)
        src = kv_all.at[r, rows, :]
        slots = ((r + 9 - 2 * y) % 8, (r + 2) % 8, (r + 6) % 8)
        copies = [
            send(src, kv_all.at[slot, rows, :], g_send.at[c, step, d], g_recv.at[c, slot], to)
            for d, (slot, to) in enumerate(zip(slots, (y_peer, up, down)))
        ]
        if to_up is not None:
            pl.when(to_up)(copies[1].start)
            pl.when(to_down)(copies[2].start)
        copies[0].start()
        return copies, to_up, to_down

    passed = []
    for c in range(4):
        rows = slice(c * quarter, (c + 1) * quarter)
        if c % 2 == 0:
            part_copies[c // 2].wait_recv()
        there = slice(c % 2 * quarter, (c % 2 + 1) * quarter)
        dk = dk_own[rows] + part_recv[c // 2, there, 0:HD].astype(jnp.float32)
        dv = dv_own[rows] + part_recv[c // 2, there, HD:].astype(jnp.float32)
        dk_ref[0, rows, :] = dk
        dv_ref[0, rows, :] = dv
        kv_all[0, rows, 0:HD] = dk.astype(jnp.bfloat16)
        kv_all[0, rows, HD:] = dv.astype(jnp.bfloat16)
        passed.append(pass_block(c, 0, 0, z < 3, z > 0))

    def arrived(c, r):
        part = kv_all.at[r, pl.ds(c * quarter, quarter), :]
        send(part, part, g_send.at[c, 0, 0], g_recv.at[c, r], y_peer).wait_recv()

    def forward_kv(step):
        r = turns[step - 1]
        rising = z >= r // 2
        for c in range(4):
            arrived(c, r)
            passed.append(
                pass_block(
                    c, step, r,
                    jnp.logical_and(rising, z < 3),
                    jnp.logical_and(jnp.logical_not(rising), z > 0),
                )
            )

    def turn_x(n):
        over_core(order[n]).wait_recv()
        xt_all[order[n]] = jnp.transpose(x_all[order[n]])

    def add(r):
        w_ref[...] += jnp.dot(xt_all[r], kv_all[r], preferred_element_type=jnp.float32)

    def add_odd(n):
        for c in range(4):
            arrived(c, odd_turns[n])
        add(odd_turns[n])

    saves[1].start()
    saves[2].start()
    for n in (1, 3, 5):
        forward_x(n)
    own_x.wait()
    xt_all[0] = jnp.transpose(x_all[0])
    w_ref[...] = jnp.dot(xt_all[0], kv_all[0], preferred_element_type=jnp.float32)
    forward_kv(1)
    for n in (0, 2, 4, 6):
        forward_x(n)
    for n in (1, 3, 5):
        forward_core(n)
    forward_kv(2)
    turn_x(1)
    add(turns[0])
    turn_x(3)
    add(turns[1])
    forward_core(0)
    forward_core(2)
    turn_x(5)
    forward_kv(3)
    forward_core(4)
    forward_core(6)
    add(turns[2])
    for n in (0, 2, 4, 6):
        turn_x(n)
        add_odd(n // 2)

    saves[3].start()
    for copy in kv_copies + part_copies:
        copy.wait_send()
    for r in range(1, 8):
        direct(r, *ring(r)).wait_send()
        over_x(r).wait_send()
        over_core(r).wait_send()
    for copies, to_up, to_down in passed:
        copies[0].wait_send()
        pl.when(to_up)(copies[1].wait_send)
        pl.when(to_down)(copies[2].wait_send)
    for copy in saves:
        copy.wait()


def write_kernel(*refs):
    sources, results, held, sem_in, sem_out = refs[:4], refs[4:8], refs[8:12], refs[12], refs[13]
    whole = [(i, slice(None)) for i in range(1, 4)]
    quarter = held[0].shape[1] // 4
    parts = whole + [(0, slice(c * quarter, (c + 1) * quarter)) for c in range(4)]
    copies = []
    for n, (i, rows) in enumerate(parts):
        at = (0, rows) if i == 0 else (slice(None),)
        copies.append((
            pltpu.make_async_copy(sources[i].at[at], held[i].at[at], sem_in.at[n]),
            pltpu.make_async_copy(held[i].at[at], results[i].at[at], sem_out.at[n]),
        ))
    for into, _ in copies:
        into.start()
    for into, out in copies:
        into.wait()
        out.start()
    for _, out in copies:
        out.wait()


def fused(inputs, queries, keys, values, outputs, out_grad, lse, positions):
    tokens = queries.shape[1]
    width = inputs.shape[2] // 8
    hbm = pl.BlockSpec(memory_space=pltpu.HBM)
    dma = pltpu.SemaphoreType.DMA
    f32, bf16 = jnp.float32, jnp.bfloat16
    lse_rows = jnp.transpose(lse, (0, 2, 1))
    args = (inputs, queries, keys, values, outputs, out_grad, lse_rows, positions)
    shapes = (
        jax.ShapeDtypeStruct(queries.shape, f32),
        jax.ShapeDtypeStruct(keys.shape, f32),
        jax.ShapeDtypeStruct(values.shape, f32),
        jax.ShapeDtypeStruct((width, 2 * HD), f32),
    )
    grads = pl.pallas_call(
        fused_kernel,
        out_shape=shapes,
        in_specs=[hbm] * 8,
        out_specs=(hbm,) * 4,
        scratch_shapes=[pltpu.VMEM(a.shape, a.dtype) for a in shapes] + [
            dma((4,)),
        ] + [pltpu.VMEM(a.shape, a.dtype) for a in args[1:]] + [
            dma((7,)),
            pltpu.VMEM((2, tokens, HD), bf16),
            pltpu.VMEM((8, tokens), jnp.int32),
            pltpu.VMEM((8, tokens), jnp.int32),
            pltpu.VMEM((queries.shape[2] // HD, HD, tokens), bf16),
            pltpu.VMEM((queries.shape[2] // HD, HD, tokens), bf16),
            pltpu.VMEM((queries.shape[2] // HD, HD, tokens), f32),
            pltpu.VMEM((8, width, tokens), bf16),
            pltpu.VMEM((2, tokens // 2, 2 * HD), bf16),
            pltpu.VMEM((2, tokens // 2, 2 * HD), bf16),
            pltpu.VMEM((8, tokens, 2 * HD), bf16),
            pltpu.VMEM((8, tokens, width), bf16),
            dma,
            dma((3,)), dma((3,)),
            dma((2,)), dma((2,)),
            dma((8,)), dma((8,)),
            dma((8,)), dma((8,)),
            dma((8,)), dma((8,)),
            dma((4, 4, 3)), dma((4, 8)),
        ],
        compiler_params=pltpu.CompilerParams(
            collective_id=0, has_side_effects=True, vmem_limit_bytes=VMEM_BYTES
        ),
    )(*args)
    return pl.pallas_call(
        write_kernel,
        out_shape=shapes,
        in_specs=[hbm] * 4,
        out_specs=(hbm,) * 4,
        scratch_shapes=[pltpu.VMEM(a.shape, a.dtype) for a in shapes] + [dma((7,)), dma((7,))],
        compiler_params=pltpu.CompilerParams(vmem_limit_bytes=VMEM_BYTES),
    )(*grads)


def fits(mesh):
    return mesh.shape["dp"] == 4 and mesh.shape["ctx"] == 2 and mesh.shape["heads"] == 4


def solution(mesh):
    return jax.shard_map(
        fused if fits(mesh) else shards,
        mesh=mesh,
        in_specs=(
            P("dp", "ctx", None),
            P("dp", "ctx", "heads"),
            P("dp", "ctx", "heads"),
            P("dp", "ctx", "heads"),
            P("dp", "ctx", "heads"),
            P("dp", "ctx", "heads"),
            P("dp", "ctx", "heads"),
            P("dp", "ctx"),
        ),
        out_specs=(
            P("dp", "ctx", "heads"),
            P("dp", "ctx", "heads"),
            P("dp", "ctx", "heads"),
            P(("dp", "ctx"), "heads"),
        ),
        check_vma=False,
    )
```

```python
import math

import jax
import jax.numpy as jnp
from jax import lax
from jax.experimental import pallas as pl
from jax.experimental.pallas import tpu as pltpu
from jax.sharding import PartitionSpec as P

HD = 128
MESH = pl.DeviceIdType.MESH
NT = (((1,), (1,)), ((), ()))
TN = (((0,), (0,)), ((), ()))
LOG2E = math.log2(math.e)
VMEM_BYTES = 60 * 1024 * 1024


def passed_along(block, axis, distance):
    devices = range(lax.axis_size(axis))
    route = [((i - distance) % len(devices), i) for i in devices]
    return lax.ppermute(block, axis, route)


def block_grads(query_blk, grad_blk, lse_blk, delta_blk, query_pos, key_blk, value_blk, key_pos):
    factor = HD ** (-0.5)
    tokens_q = query_blk.shape[0]
    tokens_k = key_blk.shape[0]
    kv_local = key_blk.shape[1] // HD
    group_size = query_blk.shape[1] // key_blk.shape[1]
    query_four = query_blk.reshape(tokens_q, kv_local, group_size, HD)
    grad_four = grad_blk.reshape(tokens_q, kv_local, group_size, HD)
    key_three = key_blk.reshape(tokens_k, kv_local, HD)
    value_three = value_blk.reshape(tokens_k, kv_local, HD)
    lse_four = jnp.transpose(lse_blk.reshape(tokens_q, kv_local, group_size), (1, 2, 0))[..., None]
    delta_four = jnp.transpose(delta_blk.reshape(tokens_q, kv_local, group_size), (1, 2, 0))[
        ..., None
    ]
    visible = key_pos[None, :] <= query_pos[:, None]
    scores = (
        jnp.einsum("qhgd,khd->hgqk", query_four, key_three, preferred_element_type=jnp.float32)
        * factor
    )
    probs = jnp.where(visible, jnp.exp(scores - lse_four), jnp.float32(0.0))
    dprobs = jnp.einsum(
        "qhgd,khd->hgqk", grad_four, value_three, preferred_element_type=jnp.float32
    )
    dscores = probs * (dprobs - delta_four)
    probs_low = probs.astype(jnp.bfloat16)
    dscores_low = dscores.astype(jnp.bfloat16)
    value_part = jnp.einsum(
        "hgqk,qhgd->khd", probs_low, grad_four, preferred_element_type=jnp.float32
    )
    key_part = (
        jnp.einsum("hgqk,qhgd->khd", dscores_low, query_four, preferred_element_type=jnp.float32)
        * factor
    )
    query_part = (
        jnp.einsum("hgqk,khd->qhgd", dscores_low, key_three, preferred_element_type=jnp.float32)
        * factor
    )
    return (
        query_part.reshape(tokens_q, kv_local * group_size * HD),
        key_part.reshape(tokens_k, kv_local * HD),
        value_part.reshape(tokens_k, kv_local * HD),
    )


def shards(inputs, queries, keys, values, outputs, out_grad, lse, positions):
    query_loc = queries[0]
    grad_loc = out_grad[0]
    key_loc = keys[0]
    value_loc = values[0]
    lse_loc = lse[0]
    tokens = query_loc.shape[0]
    heads_q = query_loc.shape[1] // HD
    kv_local = key_loc.shape[1] // HD
    delta_loc = jnp.sum(
        (grad_loc.astype(jnp.float32) * outputs[0].astype(jnp.float32)).reshape(
            tokens, heads_q, HD
        ),
        axis=2,
    )
    pos_loc = positions[0].astype(jnp.float32)
    rounds = lax.axis_size("ctx")
    zero_query = jnp.zeros((tokens, heads_q * HD), jnp.float32)
    zero_key = jnp.zeros((tokens, kv_local * HD), jnp.float32)

    def spin(index, carry):
        key_blk, value_blk, key_acc, value_acc, kpos_blk, dq_acc = carry
        query_part, key_part, value_part = block_grads(
            query_loc, grad_loc, lse_loc, delta_loc, pos_loc, key_blk, value_blk, kpos_blk
        )
        key_blk, value_blk = passed_along((key_blk, value_blk), "ctx", 1)
        key_acc, value_acc, kpos_blk = passed_along(
            (key_acc + key_part, value_acc + value_part, kpos_blk), "ctx", 1
        )
        return (key_blk, value_blk, key_acc, value_acc, kpos_blk, dq_acc + query_part)

    key_blk, value_blk, key_acc, value_acc, kpos_blk, dq_acc = lax.fori_loop(
        0, rounds - 1, spin, (key_loc, value_loc, zero_key, zero_key, pos_loc, zero_query)
    )
    query_part, key_part, value_part = block_grads(
        query_loc, grad_loc, lse_loc, delta_loc, pos_loc, key_blk, value_blk, kpos_blk
    )
    key_grad, value_grad = passed_along((key_acc + key_part, value_acc + value_part), "ctx", 1)
    query_grad = dq_acc + query_part
    kv_low = jnp.stack(
        [key_grad.reshape(tokens, kv_local, HD), value_grad.reshape(tokens, kv_local, HD)], axis=2
    )
    kv_low = kv_low.reshape(tokens, kv_local * 2 * HD).astype(jnp.bfloat16)
    inputs_loc = inputs[0]
    weight_grad = lax.psum_scatter(
        jnp.einsum("td,tc->dc", inputs_loc, kv_low, preferred_element_type=jnp.float32),
        ("dp", "ctx"),
        scatter_dimension=0,
        tiled=True,
    )
    return (query_grad[None], key_grad[None], value_grad[None], weight_grad)


def fused_kernel(
    x_ref, q_hbm, k_hbm, v_hbm, o_hbm, g_hbm, lse_hbm, pos_hbm,
    dq_hbm, dk_hbm, dv_hbm, w_hbm,
    dq_ref, dk_ref, dv_ref, w_ref, save_sem,
    q_ref, k_ref, v_ref, o_ref, g_ref, lse_ref, pos_ref, load_sem,
    kv_peer, pos_send, pos_peer, qt_ref, gt_ref, dqt_ref, wt_ref, part_send, part_recv, kv_all, x_all,
    local_sem, kv_send, kv_recv, part_ssem, part_rsem,
    xd_send, xd_recv, xx_send, xx_recv, xc_send, xc_recv, g_send, g_recv,
):
    factor = HD ** (-0.5)
    z, h, y = lax.axis_index("dp"), lax.axis_index("heads"), lax.axis_index("ctx")
    me = z * 2 + y
    heads = q_ref.shape[2] // HD
    tokens = q_ref.shape[1]
    half = tokens // 2
    quarter = tokens // 4
    width = w_ref.shape[0]
    core, xpos = h % 2, h // 2
    y_peer = {"ctx": 1 - y}
    x_peer = {"heads": (h + 2) % 4}
    core_peer = {"heads": h + 1 - 2 * core}
    rows_q = pl.ds(pl.multiple_of(half * core + quarter * xpos, quarter), quarter)
    rows_h = pl.ds(pl.multiple_of(half * core, half), half)

    def ring(r):
        other = (me + r) % 8
        return other, {"dp": other // 2, "ctx": other % 2}

    def send(src, dst, ssem, rsem, to):
        return pltpu.make_async_remote_copy(
            src_ref=src, dst_ref=dst, send_sem=ssem, recv_sem=rsem,
            device_id=to, device_id_type=MESH,
        )

    loads = [
        pltpu.make_async_copy(src, dst, load_sem.at[i])
        for i, (src, dst) in enumerate((
            (pos_hbm, pos_ref), (k_hbm, k_ref), (v_hbm, v_ref), (lse_hbm, lse_ref),
            (g_hbm, g_ref), (o_hbm, o_ref), (q_hbm, q_ref),
        ))
    ]
    for copy in loads:
        copy.start()
    barrier = pltpu.get_barrier_semaphore()
    for r in range(1, 8):
        pl.semaphore_signal(barrier, inc=1, device_id=ring(r)[1], device_id_type=MESH)
    pl.semaphore_signal(barrier, inc=1, device_id=x_peer, device_id_type=MESH)
    pl.semaphore_signal(barrier, inc=1, device_id=core_peer, device_id_type=MESH)
    own_x = pltpu.make_async_copy(
        x_ref.at[0, :, pl.ds(pl.multiple_of(me * width, 128), width)], x_all.at[0], local_sem
    )
    own_x.start()
    for copy in loads[:3]:
        copy.wait()
    pos_send[...] = jnp.broadcast_to(pos_ref[...], pos_send.shape)
    pl.semaphore_wait(barrier, 9)

    kv_copies = [
        send(k_ref.at[0], kv_peer.at[0], kv_send.at[0], kv_recv.at[0], y_peer),
        send(v_ref.at[0], kv_peer.at[1], kv_send.at[1], kv_recv.at[1], y_peer),
        send(pos_send, pos_peer, kv_send.at[2], kv_recv.at[2], y_peer),
    ]
    for copy in kv_copies:
        copy.start()
    first_z, last_z = 1 - (z + 3) // 4, z // 3
    turns = (2 + 4 * first_z, 6 - 2 * (first_z + last_z), 4 - 2 * first_z + 2 * last_z)
    odd_turns = [(r + 7 + 2 * y) % 8 for r in (0,) + turns]
    order = [r for pair in zip(odd_turns, turns) for r in pair] + odd_turns[3:]

    def direct(r, other, to):
        return send(
            x_ref.at[0, rows_q, pl.ds(pl.multiple_of(other * width, 128), width)],
            x_all.at[r, rows_q, :], xd_send.at[r], xd_recv.at[r], to,
        )

    def send_x(slots):
        for r in slots:
            back = (8 - r) % 8
            direct(back, *ring(back)).start()

    send_x(turns)

    for copy in loads[3:]:
        copy.wait()
    ones = jnp.ones((8, HD), jnp.bfloat16)
    delta = []
    for i in range(heads):
        cols = slice(i * HD, (i + 1) * HD)
        qt_ref[i] = jnp.transpose(q_ref[0, :, cols])
        gt_ref[i] = jnp.transpose(g_ref[0, :, cols])
        prod = g_ref[0, :, cols].astype(jnp.float32) * o_ref[0, :, cols].astype(jnp.float32)
        high = prod.astype(jnp.bfloat16)
        low = (prod - high.astype(jnp.float32)).astype(jnp.bfloat16)
        both = lax.dot_general(ones, high, NT, preferred_element_type=jnp.float32)
        both = both + lax.dot_general(ones, low, NT, preferred_element_type=jnp.float32)
        delta.append(both[0:1, :])
    lse_low = lse_ref[0] * LOG2E
    pos_row = pos_ref[...].astype(jnp.float32)

    def column(row):
        return jnp.transpose(jnp.broadcast_to(row, (HD, tokens)))

    def block(key, value, visible, which, sums, seen):
        key_t = jnp.transpose(key)
        dk, dv = sums
        for i in which:
            cols = slice(i * HD, (i + 1) * HD)
            scores = jnp.dot(key, qt_ref[i], preferred_element_type=jnp.float32)
            probs = jnp.exp2(scores * (factor * LOG2E) - lse_low[i:i + 1, :])
            probs = jnp.where(visible, probs, jnp.float32(0.0))
            dprobs = jnp.dot(value, gt_ref[i], preferred_element_type=jnp.float32)
            dscores = (probs * (dprobs - delta[i])).astype(jnp.bfloat16)
            probs = probs.astype(jnp.bfloat16)
            dv = dv + jnp.dot(probs, g_ref[0, :, cols], preferred_element_type=jnp.float32)
            dk = dk + jnp.dot(dscores, q_ref[0, :, cols], preferred_element_type=jnp.float32)
            dqt = jnp.dot(key_t, dscores, preferred_element_type=jnp.float32)
            if i in seen:
                dq_ref[0, :, cols] = jnp.transpose((dqt_ref[i] + dqt) * factor)
            else:
                dqt_ref[i] = dqt
        return dk, dv

    def over_x(r):
        part = x_all.at[r, rows_q, :]
        return send(part, part, xx_send.at[r], xx_recv.at[r], x_peer)

    def over_core(r):
        part = x_all.at[r, rows_h, :]
        return send(part, part, xc_send.at[r], xc_recv.at[r], core_peer)

    def forward_x(n):
        direct(order[n], *ring(order[n])).wait_recv()
        over_x(order[n]).start()

    def forward_core(n):
        over_x(order[n]).wait_recv()
        over_core(order[n]).start()

    zero = jnp.zeros((tokens, HD), jnp.float32)
    early, late = range(heads // 2), range(heads // 2, heads)
    own_sees = column(pos_row)[:, 0:1] <= pos_row
    own_sums = block(k_ref[0], v_ref[0], own_sees, early, (zero, zero), ())
    for copy in kv_copies:
        copy.wait_recv()
    send_x(odd_turns)
    peer_sees = column(pos_peer[0:1, :].astype(jnp.float32))[:, 0:1] <= pos_row
    dk, dv = block(kv_peer[0], kv_peer[1], peer_sees, range(heads), (zero, zero), early)
    dk = dk * factor
    part_copies = []
    for c in range(2):
        rows = slice(c * half, (c + 1) * half)
        part_send[c, :, 0:HD] = dk[rows].astype(jnp.bfloat16)
        part_send[c, :, HD:] = dv[rows].astype(jnp.bfloat16)
        copy = send(
            part_send.at[c], part_recv.at[c], part_ssem.at[c], part_rsem.at[c], y_peer
        )
        copy.start()
        part_copies.append(copy)
    forward_x(1)
    dk_own, dv_own = block(k_ref[0], v_ref[0], own_sees, late, own_sums, late)
    dk_own = dk_own * factor
    saves = [
        pltpu.make_async_copy(src, dst, save_sem.at[i])
        for i, (src, dst) in enumerate((
            (dq_ref, dq_hbm), (dk_ref, dk_hbm), (dv_ref, dv_hbm),
        ))
    ]
    saves[0].start()
    forward_x(3)

    up, down = {"dp": z + 1}, {"dp": z - 1}

    def pass_block(c, step, r, to_up, to_down):
        cols = slice(c * half, (c + 1) * half)
        src = kv_all.at[r, :, cols]
        slots = ((r + 9 - 2 * y) % 8, (r + 2) % 8, (r + 6) % 8)
        copies = [
            send(src, kv_all.at[slot, :, cols], g_send.at[c, step, d], g_recv.at[c, slot], to)
            for d, (slot, to) in enumerate(zip(slots, (y_peer, up, down)))
        ]
        if to_up is not None:
            pl.when(to_up)(copies[1].start)
            pl.when(to_down)(copies[2].start)
        copies[0].start()
        return copies, to_up, to_down

    passed = []
    for c in range(2):
        rows = slice(c * half, (c + 1) * half)
        part_copies[c].wait_recv()
        dk = dk_own[rows] + part_recv[c, :, 0:HD].astype(jnp.float32)
        dv = dv_own[rows] + part_recv[c, :, HD:].astype(jnp.float32)
        dk_ref[0, rows, :] = dk
        dv_ref[0, rows, :] = dv
        kv_all[0, 0:HD, rows] = jnp.transpose(dk).astype(jnp.bfloat16)
        kv_all[0, HD:, rows] = jnp.transpose(dv).astype(jnp.bfloat16)
        passed.append(pass_block(c, 0, 0, z < 3, z > 0))

    def arrived(c, r):
        part = kv_all.at[r, :, pl.ds(c * half, half)]
        send(part, part, g_send.at[c, 0, 0], g_recv.at[c, r], y_peer).wait_recv()

    def forward_kv(step):
        r = turns[step - 1]
        rising = z >= r // 2
        for c in range(2):
            arrived(c, r)
            passed.append(
                pass_block(
                    c, step, r,
                    jnp.logical_and(rising, z < 3),
                    jnp.logical_and(jnp.logical_not(rising), z > 0),
                )
            )

    def add(n):
        r = order[n]
        over_core(r).wait_recv()
        if n % 2 == 0:
            arrived(0, r)
            arrived(1, r)
        wt_ref[...] += jnp.dot(kv_all[r], x_all[r], preferred_element_type=jnp.float32)

    saves[1].start()
    saves[2].start()
    for n in (0, 5, 2):
        forward_x(n)
    forward_core(1)
    forward_core(3)
    own_x.wait()
    wt_ref[...] = jnp.dot(kv_all[0], x_all[0], preferred_element_type=jnp.float32)
    forward_x(4)
    forward_kv(1)
    forward_x(6)
    for n in (0, 5, 2):
        forward_core(n)
    add(1)
    forward_kv(2)
    forward_core(4)
    add(0)
    add(3)
    forward_kv(3)
    forward_core(6)
    for n in (2, 5, 4):
        add(n)
    r = order[6]
    over_core(r).wait_recv()
    arrived(0, r)
    arrived(1, r)
    for n in range(width // HD):
        part = slice(n * HD, (n + 1) * HD)
        term = jnp.dot(kv_all[r], x_all[r, :, part], preferred_element_type=jnp.float32)
        w_ref[part, :] = jnp.transpose(wt_ref[:, part] + term)
        saves.append(
            pltpu.make_async_copy(w_ref.at[part, :], w_hbm.at[part, :], save_sem.at[3 + n])
        )
        saves[-1].start()
    for copy in kv_copies + part_copies:
        copy.wait_send()
    for r in range(1, 8):
        direct(r, *ring(r)).wait_send()
        over_x(r).wait_send()
        over_core(r).wait_send()
    for copies, to_up, to_down in passed:
        copies[0].wait_send()
        pl.when(to_up)(copies[1].wait_send)
        pl.when(to_down)(copies[2].wait_send)
    for copy in saves:
        copy.wait()


def write_kernel(*refs):
    sources, results, held, sem_in, sem_out = refs[:4], refs[4:8], refs[8:12], refs[12], refs[13]
    whole = [(i, slice(None)) for i in range(1, 4)]
    quarter = held[0].shape[1] // 4
    parts = whole + [(0, slice(c * quarter, (c + 1) * quarter)) for c in range(4)]
    copies = []
    for n, (i, rows) in enumerate(parts):
        at = (0, rows) if i == 0 else (slice(None),)
        copies.append((
            pltpu.make_async_copy(sources[i].at[at], held[i].at[at], sem_in.at[n]),
            pltpu.make_async_copy(held[i].at[at], results[i].at[at], sem_out.at[n]),
        ))
    for into, _ in copies:
        into.start()
    for into, out in copies:
        into.wait()
        out.start()
    for _, out in copies:
        out.wait()


def fused(inputs, queries, keys, values, outputs, out_grad, lse, positions):
    tokens = queries.shape[1]
    width = inputs.shape[2] // 8
    hbm = pl.BlockSpec(memory_space=pltpu.HBM)
    dma = pltpu.SemaphoreType.DMA
    f32, bf16 = jnp.float32, jnp.bfloat16
    lse_rows = jnp.transpose(lse, (0, 2, 1))
    args = (inputs, queries, keys, values, outputs, out_grad, lse_rows, positions)
    shapes = (
        jax.ShapeDtypeStruct(queries.shape, f32),
        jax.ShapeDtypeStruct(keys.shape, f32),
        jax.ShapeDtypeStruct(values.shape, f32),
        jax.ShapeDtypeStruct((width, 2 * HD), f32),
    )
    grads = pl.pallas_call(
        fused_kernel,
        out_shape=shapes,
        in_specs=[hbm] * 8,
        out_specs=(hbm,) * 4,
        scratch_shapes=[pltpu.VMEM(a.shape, a.dtype) for a in shapes] + [
            dma((3 + width // HD,)),
        ] + [pltpu.VMEM(a.shape, a.dtype) for a in args[1:]] + [
            dma((7,)),
            pltpu.VMEM((2, tokens, HD), bf16),
            pltpu.VMEM((8, tokens), jnp.int32),
            pltpu.VMEM((8, tokens), jnp.int32),
            pltpu.VMEM((queries.shape[2] // HD, HD, tokens), bf16),
            pltpu.VMEM((queries.shape[2] // HD, HD, tokens), bf16),
            pltpu.VMEM((queries.shape[2] // HD, HD, tokens), f32),
            pltpu.VMEM((2 * HD, width), f32),
            pltpu.VMEM((2, tokens // 2, 2 * HD), bf16),
            pltpu.VMEM((2, tokens // 2, 2 * HD), bf16),
            pltpu.VMEM((8, tokens, 2 * HD), bf16),
            pltpu.VMEM((8, tokens, width), bf16),
            dma,
            dma((3,)), dma((3,)),
            dma((2,)), dma((2,)),
            dma((8,)), dma((8,)),
            dma((8,)), dma((8,)),
            dma((8,)), dma((8,)),
            dma((2, 4, 3)), dma((2, 8)),
        ],
        compiler_params=pltpu.CompilerParams(
            collective_id=0, has_side_effects=True, vmem_limit_bytes=VMEM_BYTES
        ),
    )(*args)
    return pl.pallas_call(
        write_kernel,
        out_shape=shapes,
        in_specs=[hbm] * 4,
        out_specs=(hbm,) * 4,
        scratch_shapes=[pltpu.VMEM(a.shape, a.dtype) for a in shapes] + [dma((7,)), dma((7,))],
        compiler_params=pltpu.CompilerParams(vmem_limit_bytes=VMEM_BYTES),
    )(*grads)


def fits(mesh):
    return mesh.shape["dp"] == 4 and mesh.shape["ctx"] == 2 and mesh.shape["heads"] == 4


def solution(mesh):
    return jax.shard_map(
        fused if fits(mesh) else shards,
        mesh=mesh,
        in_specs=(
            P("dp", "ctx", None),
            P("dp", "ctx", "heads"),
            P("dp", "ctx", "heads"),
            P("dp", "ctx", "heads"),
            P("dp", "ctx", "heads"),
            P("dp", "ctx", "heads"),
            P("dp", "ctx", "heads"),
            P("dp", "ctx"),
        ),
        out_specs=(
            P("dp", "ctx", "heads"),
            P("dp", "ctx", "heads"),
            P("dp", "ctx", "heads"),
            P(("dp", "ctx"), "heads"),
        ),
        check_vma=False,
    )
```

```python
import math

import jax
import jax.numpy as jnp
from jax import lax
from jax.experimental import pallas as pl
from jax.experimental.pallas import tpu as pltpu
from jax.sharding import PartitionSpec as P

HD = 128
MESH = pl.DeviceIdType.MESH
NT = (((1,), (1,)), ((), ()))
TN = (((0,), (0,)), ((), ()))
LOG2E = math.log2(math.e)
VMEM_BYTES = 60 * 1024 * 1024


def passed_along(block, axis, distance):
    devices = range(lax.axis_size(axis))
    route = [((i - distance) % len(devices), i) for i in devices]
    return lax.ppermute(block, axis, route)


def block_grads(query_blk, grad_blk, lse_blk, delta_blk, query_pos, key_blk, value_blk, key_pos):
    factor = HD ** (-0.5)
    tokens_q = query_blk.shape[0]
    tokens_k = key_blk.shape[0]
    kv_local = key_blk.shape[1] // HD
    group_size = query_blk.shape[1] // key_blk.shape[1]
    query_four = query_blk.reshape(tokens_q, kv_local, group_size, HD)
    grad_four = grad_blk.reshape(tokens_q, kv_local, group_size, HD)
    key_three = key_blk.reshape(tokens_k, kv_local, HD)
    value_three = value_blk.reshape(tokens_k, kv_local, HD)
    lse_four = jnp.transpose(lse_blk.reshape(tokens_q, kv_local, group_size), (1, 2, 0))[..., None]
    delta_four = jnp.transpose(delta_blk.reshape(tokens_q, kv_local, group_size), (1, 2, 0))[
        ..., None
    ]
    visible = key_pos[None, :] <= query_pos[:, None]
    scores = (
        jnp.einsum("qhgd,khd->hgqk", query_four, key_three, preferred_element_type=jnp.float32)
        * factor
    )
    probs = jnp.where(visible, jnp.exp(scores - lse_four), jnp.float32(0.0))
    dprobs = jnp.einsum(
        "qhgd,khd->hgqk", grad_four, value_three, preferred_element_type=jnp.float32
    )
    dscores = probs * (dprobs - delta_four)
    probs_low = probs.astype(jnp.bfloat16)
    dscores_low = dscores.astype(jnp.bfloat16)
    value_part = jnp.einsum(
        "hgqk,qhgd->khd", probs_low, grad_four, preferred_element_type=jnp.float32
    )
    key_part = (
        jnp.einsum("hgqk,qhgd->khd", dscores_low, query_four, preferred_element_type=jnp.float32)
        * factor
    )
    query_part = (
        jnp.einsum("hgqk,khd->qhgd", dscores_low, key_three, preferred_element_type=jnp.float32)
        * factor
    )
    return (
        query_part.reshape(tokens_q, kv_local * group_size * HD),
        key_part.reshape(tokens_k, kv_local * HD),
        value_part.reshape(tokens_k, kv_local * HD),
    )


def shards(inputs, queries, keys, values, outputs, out_grad, lse, positions):
    query_loc = queries[0]
    grad_loc = out_grad[0]
    key_loc = keys[0]
    value_loc = values[0]
    lse_loc = lse[0]
    tokens = query_loc.shape[0]
    heads_q = query_loc.shape[1] // HD
    kv_local = key_loc.shape[1] // HD
    delta_loc = jnp.sum(
        (grad_loc.astype(jnp.float32) * outputs[0].astype(jnp.float32)).reshape(
            tokens, heads_q, HD
        ),
        axis=2,
    )
    pos_loc = positions[0].astype(jnp.float32)
    rounds = lax.axis_size("ctx")
    zero_query = jnp.zeros((tokens, heads_q * HD), jnp.float32)
    zero_key = jnp.zeros((tokens, kv_local * HD), jnp.float32)

    def spin(index, carry):
        key_blk, value_blk, key_acc, value_acc, kpos_blk, dq_acc = carry
        query_part, key_part, value_part = block_grads(
            query_loc, grad_loc, lse_loc, delta_loc, pos_loc, key_blk, value_blk, kpos_blk
        )
        key_blk, value_blk = passed_along((key_blk, value_blk), "ctx", 1)
        key_acc, value_acc, kpos_blk = passed_along(
            (key_acc + key_part, value_acc + value_part, kpos_blk), "ctx", 1
        )
        return (key_blk, value_blk, key_acc, value_acc, kpos_blk, dq_acc + query_part)

    key_blk, value_blk, key_acc, value_acc, kpos_blk, dq_acc = lax.fori_loop(
        0, rounds - 1, spin, (key_loc, value_loc, zero_key, zero_key, pos_loc, zero_query)
    )
    query_part, key_part, value_part = block_grads(
        query_loc, grad_loc, lse_loc, delta_loc, pos_loc, key_blk, value_blk, kpos_blk
    )
    key_grad, value_grad = passed_along((key_acc + key_part, value_acc + value_part), "ctx", 1)
    query_grad = dq_acc + query_part
    kv_low = jnp.stack(
        [key_grad.reshape(tokens, kv_local, HD), value_grad.reshape(tokens, kv_local, HD)], axis=2
    )
    kv_low = kv_low.reshape(tokens, kv_local * 2 * HD).astype(jnp.bfloat16)
    inputs_loc = inputs[0]
    weight_grad = lax.psum_scatter(
        jnp.einsum("td,tc->dc", inputs_loc, kv_low, preferred_element_type=jnp.float32),
        ("dp", "ctx"),
        scatter_dimension=0,
        tiled=True,
    )
    return (query_grad[None], key_grad[None], value_grad[None], weight_grad)


def fused_kernel(
    x_ref, q_hbm, k_hbm, v_hbm, o_hbm, g_hbm, lse_hbm, pos_hbm,
    dq_hbm, dk_hbm, dv_hbm, w_hbm,
    dq_ref, dk_ref, dv_ref, w_ref, save_sem,
    q_ref, k_ref, v_ref, o_ref, g_ref, lse_ref, pos_ref, load_sem,
    kv_peer, pos_send, pos_peer, qt_ref, gt_ref, dqt_ref, wt_ref, part_send, part_recv, kv_all, x_all,
    local_sem, kv_send, kv_recv, part_ssem, part_rsem,
    xd_send, xd_recv, xx_send, xx_recv, xc_send, xc_recv, g_send, g_recv,
):
    factor = HD ** (-0.5)
    z, h, y = lax.axis_index("dp"), lax.axis_index("heads"), lax.axis_index("ctx")
    me = z * 2 + y
    heads = q_ref.shape[2] // HD
    tokens = q_ref.shape[1]
    half = tokens // 2
    quarter = tokens // 4
    width = w_ref.shape[0]
    core, xpos = h % 2, h // 2
    y_peer = {"ctx": 1 - y}
    x_peer = {"heads": (h + 2) % 4}
    core_peer = {"heads": h + 1 - 2 * core}
    rows_q = pl.ds(pl.multiple_of(half * core + quarter * xpos, quarter), quarter)
    rows_h = pl.ds(pl.multiple_of(half * core, half), half)

    def ring(r):
        other = (me + r) % 8
        return other, {"dp": other // 2, "ctx": other % 2}

    def send(src, dst, ssem, rsem, to):
        return pltpu.make_async_remote_copy(
            src_ref=src, dst_ref=dst, send_sem=ssem, recv_sem=rsem,
            device_id=to, device_id_type=MESH,
        )

    loads = [
        pltpu.make_async_copy(src, dst, load_sem.at[i])
        for i, (src, dst) in enumerate((
            (pos_hbm, pos_ref), (k_hbm, k_ref), (v_hbm, v_ref), (lse_hbm, lse_ref),
            (g_hbm, g_ref), (o_hbm, o_ref), (q_hbm, q_ref),
        ))
    ]
    for copy in loads:
        copy.start()
    barrier = pltpu.get_barrier_semaphore()
    for r in range(1, 8):
        pl.semaphore_signal(barrier, inc=1, device_id=ring(r)[1], device_id_type=MESH)
    pl.semaphore_signal(barrier, inc=1, device_id=x_peer, device_id_type=MESH)
    pl.semaphore_signal(barrier, inc=1, device_id=core_peer, device_id_type=MESH)
    own_x = pltpu.make_async_copy(
        x_ref.at[0, :, pl.ds(pl.multiple_of(me * width, 128), width)], x_all.at[0], local_sem
    )
    own_x.start()
    for copy in loads[:3]:
        copy.wait()
    pos_send[...] = jnp.broadcast_to(pos_ref[...], pos_send.shape)
    pl.semaphore_wait(barrier, 9)

    kv_copies = [
        send(k_ref.at[0], kv_peer.at[0], kv_send.at[0], kv_recv.at[0], y_peer),
        send(v_ref.at[0], kv_peer.at[1], kv_send.at[1], kv_recv.at[1], y_peer),
        send(pos_send, pos_peer, kv_send.at[2], kv_recv.at[2], y_peer),
    ]
    for copy in kv_copies:
        copy.start()
    first_z, last_z = 1 - (z + 3) // 4, z // 3
    turns = (2 + 4 * first_z, 6 - 2 * (first_z + last_z), 4 - 2 * first_z + 2 * last_z)
    odd_turns = [(r + 7 + 2 * y) % 8 for r in (0,) + turns]
    order = [r for pair in zip(odd_turns, turns) for r in pair] + odd_turns[3:]

    def direct(r, other, to):
        return send(
            x_ref.at[0, rows_q, pl.ds(pl.multiple_of(other * width, 128), width)],
            x_all.at[r, rows_q, :], xd_send.at[r], xd_recv.at[r], to,
        )

    def send_x(slots):
        for r in slots:
            back = (8 - r) % 8
            direct(back, *ring(back)).start()

    send_x(turns[::-1])

    for copy in loads[3:]:
        copy.wait()
    ones = jnp.ones((8, HD), jnp.bfloat16)
    delta = []
    for i in range(heads):
        cols = slice(i * HD, (i + 1) * HD)
        qt_ref[i] = jnp.transpose(q_ref[0, :, cols])
        gt_ref[i] = jnp.transpose(g_ref[0, :, cols])
        prod = g_ref[0, :, cols].astype(jnp.float32) * o_ref[0, :, cols].astype(jnp.float32)
        high = prod.astype(jnp.bfloat16)
        low = (prod - high.astype(jnp.float32)).astype(jnp.bfloat16)
        both = lax.dot_general(ones, high, NT, preferred_element_type=jnp.float32)
        both = both + lax.dot_general(ones, low, NT, preferred_element_type=jnp.float32)
        delta.append(both[0:1, :])
    lse_low = lse_ref[0] * LOG2E
    pos_row = pos_ref[...].astype(jnp.float32)

    def column(row):
        return jnp.transpose(jnp.broadcast_to(row, (HD, tokens)))

    def block(key, value, visible, which, sums, seen):
        key_t = jnp.transpose(key)
        dk, dv = sums
        for i in which:
            cols = slice(i * HD, (i + 1) * HD)
            scores = jnp.dot(key, qt_ref[i], preferred_element_type=jnp.float32)
            probs = jnp.exp2(scores * (factor * LOG2E) - lse_low[i:i + 1, :])
            probs = jnp.where(visible, probs, jnp.float32(0.0))
            dprobs = jnp.dot(value, gt_ref[i], preferred_element_type=jnp.float32)
            dscores = (probs * (dprobs - delta[i])).astype(jnp.bfloat16)
            probs = probs.astype(jnp.bfloat16)
            dv = dv + jnp.dot(probs, g_ref[0, :, cols], preferred_element_type=jnp.float32)
            dk = dk + jnp.dot(dscores, q_ref[0, :, cols], preferred_element_type=jnp.float32)
            dqt = jnp.dot(key_t, dscores, preferred_element_type=jnp.float32)
            if i in seen:
                dq_ref[0, :, cols] = jnp.transpose((dqt_ref[i] + dqt) * factor)
            else:
                dqt_ref[i] = dqt
        return dk, dv

    def over_x(r):
        part = x_all.at[r, rows_q, :]
        return send(part, part, xx_send.at[r], xx_recv.at[r], x_peer)

    def over_core(r):
        part = x_all.at[r, rows_h, :]
        return send(part, part, xc_send.at[r], xc_recv.at[r], core_peer)

    def forward_x(n):
        direct(order[n], *ring(order[n])).wait_recv()
        over_x(order[n]).start()

    def forward_core(n):
        over_x(order[n]).wait_recv()
        over_core(order[n]).start()

    zero = jnp.zeros((tokens, HD), jnp.float32)
    early, late = range(heads // 2), range(heads // 2, heads)
    own_sees = column(pos_row)[:, 0:1] <= pos_row
    own_sums = block(k_ref[0], v_ref[0], own_sees, early, (zero, zero), ())
    for copy in kv_copies:
        copy.wait_recv()
    send_x(odd_turns[::-1])
    peer_sees = column(pos_peer[0:1, :].astype(jnp.float32))[:, 0:1] <= pos_row
    dk, dv = block(kv_peer[0], kv_peer[1], peer_sees, range(heads), (zero, zero), early)
    dk = dk * factor
    part_copies = []
    for c in range(2):
        rows = slice(c * half, (c + 1) * half)
        part_send[c, :, 0:HD] = dk[rows].astype(jnp.bfloat16)
        part_send[c, :, HD:] = dv[rows].astype(jnp.bfloat16)
        copy = send(
            part_send.at[c], part_recv.at[c], part_ssem.at[c], part_rsem.at[c], y_peer
        )
        copy.start()
        part_copies.append(copy)
    forward_x(1)
    forward_x(3)
    dk_own, dv_own = block(k_ref[0], v_ref[0], own_sees, late, own_sums, late)
    dk_own = dk_own * factor
    saves = [
        pltpu.make_async_copy(src, dst, save_sem.at[i])
        for i, (src, dst) in enumerate((
            (dq_ref, dq_hbm), (dk_ref, dk_hbm), (dv_ref, dv_hbm),
        ))
    ]
    saves[0].start()
    forward_x(5)

    up, down = {"dp": z + 1}, {"dp": z - 1}

    def pass_block(c, step, r, to_up, to_down):
        cols = slice(c * half, (c + 1) * half)
        src = kv_all.at[r, :, cols]
        slots = ((r + 9 - 2 * y) % 8, (r + 2) % 8, (r + 6) % 8)
        copies = [
            send(src, kv_all.at[slot, :, cols], g_send.at[c, step, d], g_recv.at[c, slot], to)
            for d, (slot, to) in enumerate(zip(slots, (y_peer, up, down)))
        ]
        if to_up is not None:
            pl.when(to_up)(copies[1].start)
            pl.when(to_down)(copies[2].start)
        copies[0].start()
        return copies, to_up, to_down

    passed = []
    for c in range(2):
        rows = slice(c * half, (c + 1) * half)
        part_copies[c].wait_recv()
        dk = dk_own[rows] + part_recv[c, :, 0:HD].astype(jnp.float32)
        dv = dv_own[rows] + part_recv[c, :, HD:].astype(jnp.float32)
        dk_ref[0, rows, :] = dk
        dv_ref[0, rows, :] = dv
        kv_all[0, 0:HD, rows] = jnp.transpose(dk).astype(jnp.bfloat16)
        kv_all[0, HD:, rows] = jnp.transpose(dv).astype(jnp.bfloat16)
        passed.append(pass_block(c, 0, 0, z < 3, z > 0))

    def arrived(c, r):
        part = kv_all.at[r, :, pl.ds(c * half, half)]
        send(part, part, g_send.at[c, 0, 0], g_recv.at[c, r], y_peer).wait_recv()

    def forward_kv(step):
        r = turns[step - 1]
        rising = z >= r // 2
        for c in range(2):
            arrived(c, r)
            passed.append(
                pass_block(
                    c, step, r,
                    jnp.logical_and(rising, z < 3),
                    jnp.logical_and(jnp.logical_not(rising), z > 0),
                )
            )

    def add(n):
        r = order[n]
        over_core(r).wait_recv()
        if n % 2 == 0:
            arrived(0, r)
            arrived(1, r)
        wt_ref[...] += jnp.dot(kv_all[r], x_all[r], preferred_element_type=jnp.float32)

    saves[1].start()
    saves[2].start()
    forward_core(1)
    forward_core(3)
    own_x.wait()
    wt_ref[...] = jnp.dot(kv_all[0], x_all[0], preferred_element_type=jnp.float32)
    forward_x(0)
    forward_kv(1)
    for n in (2, 4, 6):
        forward_x(n)
    forward_core(5)
    add(1)
    forward_kv(2)
    forward_core(0)
    add(3)
    forward_kv(3)
    for n in (2, 4, 6):
        forward_core(n)
    for n in (5, 0, 2, 4):
        add(n)
    r = order[6]
    over_core(r).wait_recv()
    arrived(0, r)
    arrived(1, r)
    for n in range(width // HD):
        part = slice(n * HD, (n + 1) * HD)
        term = jnp.dot(kv_all[r], x_all[r, :, part], preferred_element_type=jnp.float32)
        w_ref[part, :] = jnp.transpose(wt_ref[:, part] + term)
        saves.append(
            pltpu.make_async_copy(w_ref.at[part, :], w_hbm.at[part, :], save_sem.at[3 + n])
        )
        saves[-1].start()
    for copy in kv_copies + part_copies:
        copy.wait_send()
    for r in range(1, 8):
        direct(r, *ring(r)).wait_send()
        over_x(r).wait_send()
        over_core(r).wait_send()
    for copies, to_up, to_down in passed:
        copies[0].wait_send()
        pl.when(to_up)(copies[1].wait_send)
        pl.when(to_down)(copies[2].wait_send)
    for copy in saves:
        copy.wait()


def write_kernel(*refs):
    sources, results, held, sem_in, sem_out = refs[:4], refs[4:8], refs[8:12], refs[12], refs[13]
    whole = [(i, slice(None)) for i in range(1, 4)]
    quarter = held[0].shape[1] // 4
    parts = whole + [(0, slice(c * quarter, (c + 1) * quarter)) for c in range(4)]
    copies = []
    for n, (i, rows) in enumerate(parts):
        at = (0, rows) if i == 0 else (slice(None),)
        copies.append((
            pltpu.make_async_copy(sources[i].at[at], held[i].at[at], sem_in.at[n]),
            pltpu.make_async_copy(held[i].at[at], results[i].at[at], sem_out.at[n]),
        ))
    for into, _ in copies:
        into.start()
    for into, out in copies:
        into.wait()
        out.start()
    for _, out in copies:
        out.wait()


def fused(inputs, queries, keys, values, outputs, out_grad, lse, positions):
    tokens = queries.shape[1]
    width = inputs.shape[2] // 8
    hbm = pl.BlockSpec(memory_space=pltpu.HBM)
    dma = pltpu.SemaphoreType.DMA
    f32, bf16 = jnp.float32, jnp.bfloat16
    lse_rows = jnp.transpose(lse, (0, 2, 1))
    args = (inputs, queries, keys, values, outputs, out_grad, lse_rows, positions)
    shapes = (
        jax.ShapeDtypeStruct(queries.shape, f32),
        jax.ShapeDtypeStruct(keys.shape, f32),
        jax.ShapeDtypeStruct(values.shape, f32),
        jax.ShapeDtypeStruct((width, 2 * HD), f32),
    )
    grads = pl.pallas_call(
        fused_kernel,
        out_shape=shapes,
        in_specs=[hbm] * 8,
        out_specs=(hbm,) * 4,
        scratch_shapes=[pltpu.VMEM(a.shape, a.dtype) for a in shapes] + [
            dma((3 + width // HD,)),
        ] + [pltpu.VMEM(a.shape, a.dtype) for a in args[1:]] + [
            dma((7,)),
            pltpu.VMEM((2, tokens, HD), bf16),
            pltpu.VMEM((8, tokens), jnp.int32),
            pltpu.VMEM((8, tokens), jnp.int32),
            pltpu.VMEM((queries.shape[2] // HD, HD, tokens), bf16),
            pltpu.VMEM((queries.shape[2] // HD, HD, tokens), bf16),
            pltpu.VMEM((queries.shape[2] // HD, HD, tokens), f32),
            pltpu.VMEM((2 * HD, width), f32),
            pltpu.VMEM((2, tokens // 2, 2 * HD), bf16),
            pltpu.VMEM((2, tokens // 2, 2 * HD), bf16),
            pltpu.VMEM((8, tokens, 2 * HD), bf16),
            pltpu.VMEM((8, tokens, width), bf16),
            dma,
            dma((3,)), dma((3,)),
            dma((2,)), dma((2,)),
            dma((8,)), dma((8,)),
            dma((8,)), dma((8,)),
            dma((8,)), dma((8,)),
            dma((2, 4, 3)), dma((2, 8)),
        ],
        compiler_params=pltpu.CompilerParams(
            collective_id=0, has_side_effects=True, vmem_limit_bytes=VMEM_BYTES
        ),
    )(*args)
    return pl.pallas_call(
        write_kernel,
        out_shape=shapes,
        in_specs=[hbm] * 4,
        out_specs=(hbm,) * 4,
        scratch_shapes=[pltpu.VMEM(a.shape, a.dtype) for a in shapes] + [dma((7,)), dma((7,))],
        compiler_params=pltpu.CompilerParams(vmem_limit_bytes=VMEM_BYTES),
    )(*grads)


def fits(mesh):
    return mesh.shape["dp"] == 4 and mesh.shape["ctx"] == 2 and mesh.shape["heads"] == 4


def solution(mesh):
    return jax.shard_map(
        fused if fits(mesh) else shards,
        mesh=mesh,
        in_specs=(
            P("dp", "ctx", None),
            P("dp", "ctx", "heads"),
            P("dp", "ctx", "heads"),
            P("dp", "ctx", "heads"),
            P("dp", "ctx", "heads"),
            P("dp", "ctx", "heads"),
            P("dp", "ctx", "heads"),
            P("dp", "ctx"),
        ),
        out_specs=(
            P("dp", "ctx", "heads"),
            P("dp", "ctx", "heads"),
            P("dp", "ctx", "heads"),
            P(("dp", "ctx"), "heads"),
        ),
        check_vma=False,
    )
```

```python
import math

import jax
import jax.numpy as jnp
from jax import lax
from jax.experimental import pallas as pl
from jax.experimental.pallas import tpu as pltpu
from jax.sharding import PartitionSpec as P

HD = 128
MESH = pl.DeviceIdType.MESH
NT = (((1,), (1,)), ((), ()))
TN = (((0,), (0,)), ((), ()))
LOG2E = math.log2(math.e)
VMEM_BYTES = 60 * 1024 * 1024


def passed_along(block, axis, distance):
    devices = range(lax.axis_size(axis))
    route = [((i - distance) % len(devices), i) for i in devices]
    return lax.ppermute(block, axis, route)


def block_grads(query_blk, grad_blk, lse_blk, delta_blk, query_pos, key_blk, value_blk, key_pos):
    factor = HD ** (-0.5)
    tokens_q = query_blk.shape[0]
    tokens_k = key_blk.shape[0]
    kv_local = key_blk.shape[1] // HD
    group_size = query_blk.shape[1] // key_blk.shape[1]
    query_four = query_blk.reshape(tokens_q, kv_local, group_size, HD)
    grad_four = grad_blk.reshape(tokens_q, kv_local, group_size, HD)
    key_three = key_blk.reshape(tokens_k, kv_local, HD)
    value_three = value_blk.reshape(tokens_k, kv_local, HD)
    lse_four = jnp.transpose(lse_blk.reshape(tokens_q, kv_local, group_size), (1, 2, 0))[..., None]
    delta_four = jnp.transpose(delta_blk.reshape(tokens_q, kv_local, group_size), (1, 2, 0))[
        ..., None
    ]
    visible = key_pos[None, :] <= query_pos[:, None]
    scores = (
        jnp.einsum("qhgd,khd->hgqk", query_four, key_three, preferred_element_type=jnp.float32)
        * factor
    )
    probs = jnp.where(visible, jnp.exp(scores - lse_four), jnp.float32(0.0))
    dprobs = jnp.einsum(
        "qhgd,khd->hgqk", grad_four, value_three, preferred_element_type=jnp.float32
    )
    dscores = probs * (dprobs - delta_four)
    probs_low = probs.astype(jnp.bfloat16)
    dscores_low = dscores.astype(jnp.bfloat16)
    value_part = jnp.einsum(
        "hgqk,qhgd->khd", probs_low, grad_four, preferred_element_type=jnp.float32
    )
    key_part = (
        jnp.einsum("hgqk,qhgd->khd", dscores_low, query_four, preferred_element_type=jnp.float32)
        * factor
    )
    query_part = (
        jnp.einsum("hgqk,khd->qhgd", dscores_low, key_three, preferred_element_type=jnp.float32)
        * factor
    )
    return (
        query_part.reshape(tokens_q, kv_local * group_size * HD),
        key_part.reshape(tokens_k, kv_local * HD),
        value_part.reshape(tokens_k, kv_local * HD),
    )


def shards(inputs, queries, keys, values, outputs, out_grad, lse, positions):
    query_loc = queries[0]
    grad_loc = out_grad[0]
    key_loc = keys[0]
    value_loc = values[0]
    lse_loc = lse[0]
    tokens = query_loc.shape[0]
    heads_q = query_loc.shape[1] // HD
    kv_local = key_loc.shape[1] // HD
    delta_loc = jnp.sum(
        (grad_loc.astype(jnp.float32) * outputs[0].astype(jnp.float32)).reshape(
            tokens, heads_q, HD
        ),
        axis=2,
    )
    pos_loc = positions[0].astype(jnp.float32)
    rounds = lax.axis_size("ctx")
    zero_query = jnp.zeros((tokens, heads_q * HD), jnp.float32)
    zero_key = jnp.zeros((tokens, kv_local * HD), jnp.float32)

    def spin(index, carry):
        key_blk, value_blk, key_acc, value_acc, kpos_blk, dq_acc = carry
        query_part, key_part, value_part = block_grads(
            query_loc, grad_loc, lse_loc, delta_loc, pos_loc, key_blk, value_blk, kpos_blk
        )
        key_blk, value_blk = passed_along((key_blk, value_blk), "ctx", 1)
        key_acc, value_acc, kpos_blk = passed_along(
            (key_acc + key_part, value_acc + value_part, kpos_blk), "ctx", 1
        )
        return (key_blk, value_blk, key_acc, value_acc, kpos_blk, dq_acc + query_part)

    key_blk, value_blk, key_acc, value_acc, kpos_blk, dq_acc = lax.fori_loop(
        0, rounds - 1, spin, (key_loc, value_loc, zero_key, zero_key, pos_loc, zero_query)
    )
    query_part, key_part, value_part = block_grads(
        query_loc, grad_loc, lse_loc, delta_loc, pos_loc, key_blk, value_blk, kpos_blk
    )
    key_grad, value_grad = passed_along((key_acc + key_part, value_acc + value_part), "ctx", 1)
    query_grad = dq_acc + query_part
    kv_low = jnp.stack(
        [key_grad.reshape(tokens, kv_local, HD), value_grad.reshape(tokens, kv_local, HD)], axis=2
    )
    kv_low = kv_low.reshape(tokens, kv_local * 2 * HD).astype(jnp.bfloat16)
    inputs_loc = inputs[0]
    weight_grad = lax.psum_scatter(
        jnp.einsum("td,tc->dc", inputs_loc, kv_low, preferred_element_type=jnp.float32),
        ("dp", "ctx"),
        scatter_dimension=0,
        tiled=True,
    )
    return (query_grad[None], key_grad[None], value_grad[None], weight_grad)


def fused_kernel(
    x_ref, q_hbm, k_hbm, v_hbm, o_hbm, g_hbm, lse_hbm, pos_hbm,
    dq_hbm, dk_hbm, dv_hbm, w_hbm,
    dq_ref, dk_ref, dv_ref, w_ref, save_sem,
    q_ref, k_ref, v_ref, o_ref, g_ref, lse_ref, pos_ref, load_sem,
    kv_peer, pos_send, pos_peer, qt_ref, gt_ref, dqt_ref, wt_ref, part_send, part_recv, kv_all, x_all,
    local_sem, kv_send, kv_recv, part_ssem, part_rsem,
    xd_send, xd_recv, xx_send, xx_recv, xc_send, xc_recv, g_send, g_recv,
):
    factor = HD ** (-0.5)
    z, h, y = lax.axis_index("dp"), lax.axis_index("heads"), lax.axis_index("ctx")
    me = z * 2 + y
    heads = q_ref.shape[2] // HD
    tokens = q_ref.shape[1]
    half = tokens // 2
    quarter = tokens // 4
    width = w_ref.shape[0]
    core, xpos = h % 2, h // 2
    y_peer = {"ctx": 1 - y}
    x_peer = {"heads": (h + 2) % 4}
    core_peer = {"heads": h + 1 - 2 * core}
    rows_q = pl.ds(pl.multiple_of(half * core + quarter * xpos, quarter), quarter)
    rows_h = pl.ds(pl.multiple_of(half * core, half), half)

    def ring(r):
        other = (me + r) % 8
        return other, {"dp": other // 2, "ctx": other % 2}

    def send(src, dst, ssem, rsem, to):
        return pltpu.make_async_remote_copy(
            src_ref=src, dst_ref=dst, send_sem=ssem, recv_sem=rsem,
            device_id=to, device_id_type=MESH,
        )

    loads = [
        pltpu.make_async_copy(src, dst, load_sem.at[i])
        for i, (src, dst) in enumerate((
            (pos_hbm, pos_ref), (k_hbm, k_ref), (v_hbm, v_ref), (lse_hbm, lse_ref),
            (g_hbm, g_ref), (o_hbm, o_ref), (q_hbm, q_ref),
        ))
    ]
    for copy in loads:
        copy.start()
    barrier = pltpu.get_barrier_semaphore()
    for r in range(1, 8):
        pl.semaphore_signal(barrier, inc=1, device_id=ring(r)[1], device_id_type=MESH)
    pl.semaphore_signal(barrier, inc=1, device_id=x_peer, device_id_type=MESH)
    pl.semaphore_signal(barrier, inc=1, device_id=core_peer, device_id_type=MESH)
    own_x = pltpu.make_async_copy(
        x_ref.at[0, :, pl.ds(pl.multiple_of(me * width, 128), width)], x_all.at[0], local_sem
    )
    own_x.start()
    for copy in loads[:3]:
        copy.wait()
    pos_send[...] = jnp.broadcast_to(pos_ref[...], pos_send.shape)
    pl.semaphore_wait(barrier, 9)

    kv_copies = [
        send(k_ref.at[0], kv_peer.at[0], kv_send.at[0], kv_recv.at[0], y_peer),
        send(v_ref.at[0], kv_peer.at[1], kv_send.at[1], kv_recv.at[1], y_peer),
        send(pos_send, pos_peer, kv_send.at[2], kv_recv.at[2], y_peer),
    ]
    for copy in kv_copies:
        copy.start()
    first_z, last_z = 1 - (z + 3) // 4, z // 3
    turns = (2 + 4 * first_z, 6 - 2 * (first_z + last_z), 4 - 2 * first_z + 2 * last_z)
    odd_turns = [(r + 7 + 2 * y) % 8 for r in (0,) + turns]
    order = [r for pair in zip(odd_turns, turns) for r in pair] + odd_turns[3:]

    def direct(r, other, to):
        return send(
            x_ref.at[0, rows_q, pl.ds(pl.multiple_of(other * width, 128), width)],
            x_all.at[r, rows_q, :], xd_send.at[r], xd_recv.at[r], to,
        )

    def send_x(slots):
        for r in slots:
            back = (8 - r) % 8
            direct(back, *ring(back)).start()

    send_x(turns[::-1] + tuple(odd_turns[:1:-1]))

    for copy in loads[3:]:
        copy.wait()
    ones = jnp.ones((8, HD), jnp.bfloat16)
    delta = []
    for i in range(heads):
        cols = slice(i * HD, (i + 1) * HD)
        qt_ref[i] = jnp.transpose(q_ref[0, :, cols])
        gt_ref[i] = jnp.transpose(g_ref[0, :, cols])
        prod = g_ref[0, :, cols].astype(jnp.float32) * o_ref[0, :, cols].astype(jnp.float32)
        high = prod.astype(jnp.bfloat16)
        low = (prod - high.astype(jnp.float32)).astype(jnp.bfloat16)
        both = lax.dot_general(ones, high, NT, preferred_element_type=jnp.float32)
        both = both + lax.dot_general(ones, low, NT, preferred_element_type=jnp.float32)
        delta.append(both[0:1, :])
    lse_low = lse_ref[0] * LOG2E
    pos_row = pos_ref[...].astype(jnp.float32)

    def column(row):
        return jnp.transpose(jnp.broadcast_to(row, (HD, tokens)))

    def block(key, value, visible, which, sums, seen):
        key_t = jnp.transpose(key)
        dk, dv = sums
        for i in which:
            cols = slice(i * HD, (i + 1) * HD)
            scores = jnp.dot(key, qt_ref[i], preferred_element_type=jnp.float32)
            probs = jnp.exp2(scores * (factor * LOG2E) - lse_low[i:i + 1, :])
            probs = jnp.where(visible, probs, jnp.float32(0.0))
            dprobs = jnp.dot(value, gt_ref[i], preferred_element_type=jnp.float32)
            dscores = (probs * (dprobs - delta[i])).astype(jnp.bfloat16)
            probs = probs.astype(jnp.bfloat16)
            dv = dv + jnp.dot(probs, g_ref[0, :, cols], preferred_element_type=jnp.float32)
            dk = dk + jnp.dot(dscores, q_ref[0, :, cols], preferred_element_type=jnp.float32)
            dqt = jnp.dot(key_t, dscores, preferred_element_type=jnp.float32)
            if i in seen:
                dq_ref[0, :, cols] = jnp.transpose((dqt_ref[i] + dqt) * factor)
            else:
                dqt_ref[i] = dqt
        return dk, dv

    def over_x(r):
        part = x_all.at[r, rows_q, :]
        return send(part, part, xx_send.at[r], xx_recv.at[r], x_peer)

    def over_core(r):
        part = x_all.at[r, rows_h, :]
        return send(part, part, xc_send.at[r], xc_recv.at[r], core_peer)

    def forward_x(n):
        direct(order[n], *ring(order[n])).wait_recv()
        over_x(order[n]).start()

    def forward_core(n):
        over_x(order[n]).wait_recv()
        over_core(order[n]).start()

    zero = jnp.zeros((tokens, HD), jnp.float32)
    early, late = range(heads // 2), range(heads // 2, heads)
    own_sees = column(pos_row)[:, 0:1] <= pos_row
    own_sums = block(k_ref[0], v_ref[0], own_sees, early, (zero, zero), ())
    for copy in kv_copies:
        copy.wait_recv()
    send_x(odd_turns[1::-1])
    peer_sees = column(pos_peer[0:1, :].astype(jnp.float32))[:, 0:1] <= pos_row
    dk, dv = block(kv_peer[0], kv_peer[1], peer_sees, range(heads), (zero, zero), early)
    dk = dk * factor
    part_copies = []
    for c in range(2):
        rows = slice(c * half, (c + 1) * half)
        part_send[c, :, 0:HD] = dk[rows].astype(jnp.bfloat16)
        part_send[c, :, HD:] = dv[rows].astype(jnp.bfloat16)
        copy = send(
            part_send.at[c], part_recv.at[c], part_ssem.at[c], part_rsem.at[c], y_peer
        )
        copy.start()
        part_copies.append(copy)
    forward_x(1)
    forward_x(3)
    dk_own, dv_own = block(k_ref[0], v_ref[0], own_sees, late, own_sums, late)
    dk_own = dk_own * factor
    saves = [
        pltpu.make_async_copy(src, dst, save_sem.at[i])
        for i, (src, dst) in enumerate((
            (dq_ref, dq_hbm), (dk_ref, dk_hbm), (dv_ref, dv_hbm),
        ))
    ]
    saves[0].start()
    forward_x(5)

    up, down = {"dp": z + 1}, {"dp": z - 1}

    def pass_block(c, step, r, to_up, to_down):
        cols = slice(c * half, (c + 1) * half)
        src = kv_all.at[r, :, cols]
        slots = ((r + 9 - 2 * y) % 8, (r + 2) % 8, (r + 6) % 8)
        copies = [
            send(src, kv_all.at[slot, :, cols], g_send.at[c, step, d], g_recv.at[c, slot], to)
            for d, (slot, to) in enumerate(zip(slots, (y_peer, up, down)))
        ]
        if to_up is not None:
            pl.when(to_up)(copies[1].start)
            pl.when(to_down)(copies[2].start)
        copies[0].start()
        return copies, to_up, to_down

    passed = []
    for c in range(2):
        rows = slice(c * half, (c + 1) * half)
        part_copies[c].wait_recv()
        dk = dk_own[rows] + part_recv[c, :, 0:HD].astype(jnp.float32)
        dv = dv_own[rows] + part_recv[c, :, HD:].astype(jnp.float32)
        dk_ref[0, rows, :] = dk
        dv_ref[0, rows, :] = dv
        kv_all[0, 0:HD, rows] = jnp.transpose(dk).astype(jnp.bfloat16)
        kv_all[0, HD:, rows] = jnp.transpose(dv).astype(jnp.bfloat16)
        passed.append(pass_block(c, 0, 0, z < 3, z > 0))

    def arrived(c, r):
        part = kv_all.at[r, :, pl.ds(c * half, half)]
        send(part, part, g_send.at[c, 0, 0], g_recv.at[c, r], y_peer).wait_recv()

    def forward_kv(step):
        r = turns[step - 1]
        rising = z >= r // 2
        for c in range(2):
            arrived(c, r)
            passed.append(
                pass_block(
                    c, step, r,
                    jnp.logical_and(rising, z < 3),
                    jnp.logical_and(jnp.logical_not(rising), z > 0),
                )
            )

    def add(n):
        r = order[n]
        over_core(r).wait_recv()
        if n % 2 == 0:
            arrived(0, r)
            arrived(1, r)
        wt_ref[...] += jnp.dot(kv_all[r], x_all[r], preferred_element_type=jnp.float32)

    saves[1].start()
    saves[2].start()
    forward_core(1)
    forward_core(3)
    own_x.wait()
    wt_ref[...] = jnp.dot(kv_all[0], x_all[0], preferred_element_type=jnp.float32)
    forward_x(0)
    forward_kv(1)
    for n in (2, 4, 6):
        forward_x(n)
    forward_core(5)
    add(1)
    forward_kv(2)
    forward_core(0)
    add(3)
    forward_core(2)
    forward_kv(3)
    for n in (4, 6):
        forward_core(n)
    for n in (5, 0, 2, 4):
        add(n)
    r = order[6]
    over_core(r).wait_recv()
    arrived(0, r)
    arrived(1, r)
    for n in range(width // HD):
        part = slice(n * HD, (n + 1) * HD)
        term = jnp.dot(kv_all[r], x_all[r, :, part], preferred_element_type=jnp.float32)
        w_ref[part, :] = jnp.transpose(wt_ref[:, part] + term)
        saves.append(
            pltpu.make_async_copy(w_ref.at[part, :], w_hbm.at[part, :], save_sem.at[3 + n])
        )
        saves[-1].start()
    for copy in kv_copies + part_copies:
        copy.wait_send()
    for r in range(1, 8):
        direct(r, *ring(r)).wait_send()
        over_x(r).wait_send()
        over_core(r).wait_send()
    for copies, to_up, to_down in passed:
        copies[0].wait_send()
        pl.when(to_up)(copies[1].wait_send)
        pl.when(to_down)(copies[2].wait_send)
    for copy in saves:
        copy.wait()


def write_kernel(*refs):
    sources, results, held, sem_in, sem_out = refs[:4], refs[4:8], refs[8:12], refs[12], refs[13]
    whole = [(i, slice(None)) for i in range(1, 4)]
    quarter = held[0].shape[1] // 4
    parts = whole + [(0, slice(c * quarter, (c + 1) * quarter)) for c in range(4)]
    copies = []
    for n, (i, rows) in enumerate(parts):
        at = (0, rows) if i == 0 else (slice(None),)
        copies.append((
            pltpu.make_async_copy(sources[i].at[at], held[i].at[at], sem_in.at[n]),
            pltpu.make_async_copy(held[i].at[at], results[i].at[at], sem_out.at[n]),
        ))
    for into, _ in copies:
        into.start()
    for into, out in copies:
        into.wait()
        out.start()
    for _, out in copies:
        out.wait()


def fused(inputs, queries, keys, values, outputs, out_grad, lse, positions):
    tokens = queries.shape[1]
    width = inputs.shape[2] // 8
    hbm = pl.BlockSpec(memory_space=pltpu.HBM)
    dma = pltpu.SemaphoreType.DMA
    f32, bf16 = jnp.float32, jnp.bfloat16
    lse_rows = jnp.transpose(lse, (0, 2, 1))
    args = (inputs, queries, keys, values, outputs, out_grad, lse_rows, positions)
    shapes = (
        jax.ShapeDtypeStruct(queries.shape, f32),
        jax.ShapeDtypeStruct(keys.shape, f32),
        jax.ShapeDtypeStruct(values.shape, f32),
        jax.ShapeDtypeStruct((width, 2 * HD), f32),
    )
    grads = pl.pallas_call(
        fused_kernel,
        out_shape=shapes,
        in_specs=[hbm] * 8,
        out_specs=(hbm,) * 4,
        scratch_shapes=[pltpu.VMEM(a.shape, a.dtype) for a in shapes] + [
            dma((3 + width // HD,)),
        ] + [pltpu.VMEM(a.shape, a.dtype) for a in args[1:]] + [
            dma((7,)),
            pltpu.VMEM((2, tokens, HD), bf16),
            pltpu.VMEM((8, tokens), jnp.int32),
            pltpu.VMEM((8, tokens), jnp.int32),
            pltpu.VMEM((queries.shape[2] // HD, HD, tokens), bf16),
            pltpu.VMEM((queries.shape[2] // HD, HD, tokens), bf16),
            pltpu.VMEM((queries.shape[2] // HD, HD, tokens), f32),
            pltpu.VMEM((2 * HD, width), f32),
            pltpu.VMEM((2, tokens // 2, 2 * HD), bf16),
            pltpu.VMEM((2, tokens // 2, 2 * HD), bf16),
            pltpu.VMEM((8, tokens, 2 * HD), bf16),
            pltpu.VMEM((8, tokens, width), bf16),
            dma,
            dma((3,)), dma((3,)),
            dma((2,)), dma((2,)),
            dma((8,)), dma((8,)),
            dma((8,)), dma((8,)),
            dma((8,)), dma((8,)),
            dma((2, 4, 3)), dma((2, 8)),
        ],
        compiler_params=pltpu.CompilerParams(
            collective_id=0, has_side_effects=True, vmem_limit_bytes=VMEM_BYTES
        ),
    )(*args)
    return pl.pallas_call(
        write_kernel,
        out_shape=shapes,
        in_specs=[hbm] * 4,
        out_specs=(hbm,) * 4,
        scratch_shapes=[pltpu.VMEM(a.shape, a.dtype) for a in shapes] + [dma((7,)), dma((7,))],
        compiler_params=pltpu.CompilerParams(vmem_limit_bytes=VMEM_BYTES),
    )(*grads)


def fits(mesh):
    return mesh.shape["dp"] == 4 and mesh.shape["ctx"] == 2 and mesh.shape["heads"] == 4


def solution(mesh):
    return jax.shard_map(
        fused if fits(mesh) else shards,
        mesh=mesh,
        in_specs=(
            P("dp", "ctx", None),
            P("dp", "ctx", "heads"),
            P("dp", "ctx", "heads"),
            P("dp", "ctx", "heads"),
            P("dp", "ctx", "heads"),
            P("dp", "ctx", "heads"),
            P("dp", "ctx", "heads"),
            P("dp", "ctx"),
        ),
        out_specs=(
            P("dp", "ctx", "heads"),
            P("dp", "ctx", "heads"),
            P("dp", "ctx", "heads"),
            P(("dp", "ctx"), "heads"),
        ),
        check_vma=False,
    )
```
